256 devices in a mesh: ctx: 8 (over x_lo, y), fsdp: 16 (over z, x_hi), dp: 2 (over core).
Axes of the slice: x: 4 (x_hi: 2, x_lo: 2; x = x_hi * 2 + x_lo), y: 4, z: 8, core: 2. Of those that a mesh axis runs over, the one named last changes fastest.
Arguments:
- frames: bfloat16 [32, 1024, 1536], P(('dp', 'fsdp'), 'ctx'), parts along dimension 0, may hold values from -6 to 6
- lengths: int32 [32], P(('dp', 'fsdp')), parts along dimension 0, may hold values from 256 to 1024, as said below
- w_qkv: bfloat16 [1536, 2304], P('fsdp'), may hold values from -2.5 to 2.5
- w_out: bfloat16 [768, 1536], P('fsdp'), may hold values from -0.21875 to 0.21875
- w_glu: bfloat16 [1536, 3072], P('fsdp'), may hold values from -0.15625 to 0.15625
- depth_kernel: bfloat16 [31, 1536], replicated, may hold values from -1 to 1
- w_conv_out: bfloat16 [1536, 1536], P('fsdp'), may hold values from -0.15625 to 0.15625
Outputs:
- block_out: bfloat16 [32, 1024, 1536], P(('dp', 'fsdp'), 'ctx'), parts along dimension 0
The draws below stay inside these ranges and needn't reach their ends.
There are 2 independent parts, one for each index of `dp`. The reference program is written for one: setup_inputs(seed, part) draws one part's arguments, and reference() takes and returns one part's arrays. A program takes and returns all parts, laid end to end along the dimension named above; an argument that names none is the same for every part. Nothing has to cross between parts.
Inputs may be any that keep to these rules, and one draw needn't show every extreme that they name: `lengths`: valid frames of each recording; in every draw some recording has all 1024 frames valid.
All inputs are finite; a program needn't handle non-finite values.
Results may differ from the reference program's by a relative error of at most 0.012.
Values may be sent and summed in bfloat16 or wider, within the bound.
No kernel may reach another device: no remote copies, remote signals or barrier semaphores. Data moves between devices by JAX's collectives and lax.ppermute only.
A program may use at most 64 MiB of HBM per device.

```python
import math
import jax
import jax.numpy as jnp
from jax import lax

D = 1536
HEADS = 8
DH = 96
TAPS = 31
FR_DEV = 128
SEQ = 1024
RECS = 16


def draw_lengths(key, part):
    key = jax.random.fold_in(key, 11)
    first, second = jax.random.split(key)
    drawn = jax.random.randint(first, (RECS,), SEQ // 4, SEQ + 1)
    full_index = jax.random.randint(second, (), 0, RECS)
    return jnp.where(jnp.arange(RECS) == full_index, SEQ, drawn).astype(jnp.int32)


def draw_w_qkv(key, part):
    key = jax.random.fold_in(key, 23)
    first = jax.random.fold_in(key, 0)
    width = HEADS * DH
    normal_part = jnp.clip(jax.random.normal(first, (D, 3 * width), jnp.float32), -6.0, 6.0) * (2.0 / math.sqrt(D))
    return jnp.clip(normal_part, -2.5, 2.5).astype(jnp.bfloat16)


def block_scale(key, shape, pieces, smallest, high):
    loudness, own = 1.0, jax.random.fold_in(key, 6)
    for position, parts in pieces:
        steps = jnp.exp(jax.random.uniform(jax.random.fold_in(own, position), (parts,), jnp.float32, smallest / len(pieces), high / len(pieces)))
        loudness = loudness * jnp.repeat(steps, shape[position] // parts).reshape([-1 if axis == position else 1 for axis in range(len(shape))])
    return loudness


def centred(stream_key, shape, scale, most, cuts=(), dtype=jnp.bfloat16):
    gain = block_scale(stream_key, shape, cuts, -0.22, 0.18) if cuts else 1.0
    entries = jax.random.normal(stream_key, shape, jnp.float32) * scale * gain
    return jnp.minimum(jnp.maximum(entries, -most), most).astype(dtype)


def setup_inputs(seed: int = 0, part: int = 0) -> dict:
    arg_keys = jax.random.split(jax.random.key(seed), 8)
    own_keys = jax.random.split(jax.random.fold_in(arg_keys[7], part), 8)
    return {
        "frames": centred(own_keys[0], (RECS, SEQ, D), 1.0, 6.0, ((0, 16), (1, 8))),
        "lengths": draw_lengths(jax.random.fold_in(jax.random.fold_in(arg_keys[7], part), 71), part),
        "w_qkv": draw_w_qkv(jax.random.fold_in(arg_keys[7], 71), part),
        "w_out": centred(arg_keys[3], (HEADS * DH, D), (HEADS * DH) ** -0.5, 0.21875, ((0, 16),)),
        "w_glu": centred(arg_keys[4], (D, 2 * D), D ** -0.5, 0.15625, ((0, 16),)),
        "depth_kernel": centred(arg_keys[5], (TAPS, D), TAPS ** -0.5, 1.0),
        "w_conv_out": centred(arg_keys[6], (D, D), D ** -0.5, 0.15625, ((0, 16),)),
    }


masked_score = -1e+30

def layer_norm(values):
    middle = lax.optimization_barrier(jnp.mean(values, axis=-1, keepdims=True))
    spread = lax.optimization_barrier(jnp.mean((values - middle) ** 2, axis=-1, keepdims=True))
    return (values - middle) * lax.rsqrt(spread + 1e-05)

def attend(query_rows, key_rows, value_rows, length, block):
    total_rows = key_rows.shape[0]
    valid = jnp.arange(total_rows) < length
    key_float = key_rows.astype(jnp.float32)
    value_float = value_rows.astype(jnp.float32)
    blocks = query_rows.reshape(total_rows // block, block, HEADS, DH)

    def one_block(query_block):
        scores = jnp.einsum('qhd,khd->hqk', query_block.astype(jnp.float32), key_float) * DH ** (-0.5)
        scores = jnp.where(valid[None, None, :], scores, masked_score)
        row_max = lax.optimization_barrier(jnp.max(scores, axis=-1, keepdims=True))
        exp_scores = jnp.exp(scores - row_max)
        row_total = lax.optimization_barrier(jnp.sum(exp_scores, axis=-1))
        exp_rounded = lax.optimization_barrier(exp_scores.astype(jnp.bfloat16))
        summed = jnp.einsum('hqk,khd->qhd', exp_rounded.astype(jnp.float32), value_float)
        return (summed / jnp.transpose(row_total)[:, :, None]).astype(jnp.bfloat16)
    return lax.map(one_block, blocks).reshape(total_rows, HEADS * DH)

def reference(frames, lengths, w_qkv, w_out, w_glu, depth_kernel, w_conv_out):
    width = HEADS * DH
    half_taps = TAPS // 2

    def one_recording(inputs):
        frame_rows, length = inputs
        normed = layer_norm(frame_rows.astype(jnp.float32)).astype(jnp.bfloat16)
        qkv = jnp.dot(normed, w_qkv, preferred_element_type=jnp.float32).astype(jnp.bfloat16)
        query_rows = qkv[:, :width].reshape(SEQ, HEADS, DH)
        key_rows = qkv[:, width:2 * width].reshape(SEQ, HEADS, DH)
        value_rows = qkv[:, 2 * width:].reshape(SEQ, HEADS, DH)
        attended = attend(query_rows, key_rows, value_rows, length, FR_DEV)
        mixed = (frame_rows.astype(jnp.float32) + jnp.dot(attended, w_out, preferred_element_type=jnp.float32)).astype(jnp.bfloat16)
        renormed = layer_norm(mixed.astype(jnp.float32)).astype(jnp.bfloat16)
        glu_in = jnp.dot(renormed, w_glu, preferred_element_type=jnp.float32)
        gated = glu_in[:, :D] * jax.nn.sigmoid(glu_in[:, D:])
        valid = jnp.arange(SEQ) < length
        gated = jnp.where(valid[:, None], gated, jnp.float32(0.0)).astype(jnp.bfloat16)
        padded = jnp.pad(gated.astype(jnp.float32), ((half_taps, half_taps), (0, 0)))
        kernel = depth_kernel.astype(jnp.float32)
        conv_sum = jnp.zeros((SEQ, D), jnp.float32)
        for tap_index in range(TAPS):
            conv_sum = conv_sum + kernel[tap_index][None, :] * padded[tap_index:tap_index + SEQ]
        activated = jax.nn.silu(layer_norm(conv_sum)).astype(jnp.bfloat16)
        result = mixed.astype(jnp.float32) + jnp.dot(activated, w_conv_out, preferred_element_type=jnp.float32)
        return result.astype(jnp.bfloat16)
    return lax.map(one_recording, (frames, lengths))
```

```python
import numpy as np
import jax
import jax.numpy as jnp
from jax import lax
from jax.experimental import pallas as pl
from jax.experimental.pallas import tpu as pltpu
from jax.sharding import PartitionSpec as P

HEADS = 8
DH = 96
TAPS = 31
D = 1536
ROWS = 128
SEQ = 1024
LANES = 128
masked_score = -1e30

AXES = ("ctx", "fsdp", "dp")
SHAPE = (2, 4, 8, 2, 2)
F32 = jnp.float32
BF16 = jnp.bfloat16


def pairs(move):
    out = []
    for i in range(256):
        c = [int(v) for v in np.unravel_index(i, SHAPE)]
        out.append((i, int(np.ravel_multi_index(move(*c), SHAPE))))
    return out


def xor_y(k):
    return pairs(lambda a, y, z, h, c: (a, y ^ k, z, h, c))


def xor_x(k):
    return pairs(lambda a, y, z, h, c: (a ^ (k & 1), y, z, h ^ (k >> 1), c))


def shift_y(k):
    return pairs(lambda a, y, z, h, c: (a, (y + k) % 4, z, h, c))


def shift_z(k):
    return pairs(lambda a, y, z, h, c: (a, y, (z + k) % 8, h, c))


SWAP_CORE = pairs(lambda a, y, z, h, c: (a, y, z, h, 1 - c))
SWAP_H = pairs(lambda a, y, z, h, c: (a, y, z, 1 - h, c))
SWAP_A = pairs(lambda a, y, z, h, c: (1 - a, y, z, h, c))
Z_GROUPS = [
    [int(np.ravel_multi_index((a, y, z, h, c), SHAPE)) for z in range(8)]
    for a in range(2) for y in range(4) for h in range(2) for c in range(2)
]


def send(value, moves):
    return lax.ppermute(value, AXES, moves)


def params(mib=48):
    return pltpu.CompilerParams(vmem_limit_bytes=mib * 2**20)


VM = pl.BlockSpec(memory_space=pltpu.VMEM)
SM = pl.BlockSpec(memory_space=pltpu.SMEM)
ANY = pl.BlockSpec(memory_space=pl.ANY)


def norm_rows(values):
    middle = jnp.mean(values, axis=-1, keepdims=True)
    apart = values - middle
    spread = jnp.mean(apart * apart, axis=-1, keepdims=True)
    return apart * lax.rsqrt(spread + 1e-05)


def pack_kernel(place, w_qkv, w_out, w_glu, w_conv, hp, gam_a, gam_b):
    ctx, y, a, core = place[0], place[1], place[2], place[5]
    zero = jnp.zeros((288, LANES), BF16)
    hp[0:288, :] = zero
    for j in range(HEADS):

        @pl.when(ctx == j)
        def _():
            for part in range(3):
                first = part * 768 + DH * j
                hp[96 * part : 96 * (part + 1), 0:DH] = w_qkv[:, first : first + DH]

    def block(ref, index):
        return ref[:, pl.ds(pl.multiple_of(index * LANES, LANES), LANES)]

    hp[288:336, :] = block(w_out, core * 6 + y)
    hp[336:432, :] = block(w_glu, core * 12 + y)
    hp[432:528, :] = block(w_conv, core * 6 + y)
    gam_a[0:48, :] = block(w_out, core * 6 + 4 + a)
    for j in range(2):
        gam_a[48 + 96 * j : 144 + 96 * j, :] = block(w_glu, core * 12 + 4 + a * 4 + j)
        gam_b[96 + 96 * j : 192 + 96 * j, :] = block(w_glu, core * 12 + 6 + a * 4 + j)
    gam_b[0:96, :] = block(w_conv, core * 6 + 4 + a)


def join_kernel(place, own, other, gam_a, gam_b, q, pack_a, pack_b):
    h = place[4]
    for ref, at in ((own, h), (other, 1 - h)):
        q[at] = ref[0:288, :]
        pack_a[pl.ds(pl.multiple_of(at * 144, 16), 144), :] = ref[288:432, :]
        pack_b[pl.ds(pl.multiple_of(at * 96, 16), 96), :] = ref[432:528, :]
    pack_a[288:528, :] = gam_a[...]
    pack_b[192:480, :] = gam_b[...]


def norm_kernel(x, out):
    out[...] = norm_rows(x[...].astype(F32)).astype(BF16)


def run_copies(copies, sems):
    made = [pltpu.make_async_copy(src, dst, sems.at[i]) for i, (src, dst) in enumerate(copies)]
    for copy in made:
        copy.start()

    def wait():
        for copy in made:
            copy.wait()

    return wait


def attend_kernel(place, length, *refs):
    front, back, weights = refs[0:4], refs[4:6], refs[6:14]
    out, x, w, q, k, v, sems = refs[14:]
    y, a, z = place[1], place[2], place[3]
    copies = []
    order = (0, -1, 1, -2)
    for i, k_y in enumerate(order):
        at = (y + k_y + 4) % 4
        for side in range(2):
            there = a if side == 0 else 1 - a
            copies.append((front[i].at[side], x.at[there * 4 + at, 0]))
            copies.append((back[side].at[i], x.at[there * 4 + at, 1]))
    for i in range(8):
        at = (z - i + 8) % 8
        for part in range(3):
            copies.append(
                (weights[i].at[:, 96 * part : 96 * (part + 1), :],
                 w.at[at, :, :, LANES * part : LANES * (part + 1)])
            )
    run_copies(copies, sems)()
    rows = x[...].reshape(SEQ, D)
    for part, ref in enumerate((q, k, v)):
        mat = w[:, :, :, LANES * part : LANES * (part + 1)].reshape(D, LANES)
        ref[...] = jnp.dot(rows, mat, preferred_element_type=F32).astype(BF16)
    valid = lax.broadcasted_iota(jnp.int32, (1, SEQ), 1) < length[0]
    keys, values = k[...], v[...]
    for i in range(HEADS):
        scores = lax.dot_general(
            q[ROWS * i : ROWS * (i + 1), :], keys, (((1,), (1,)), ((), ())), preferred_element_type=F32
        ) * DH ** (-0.5)
        scores = jnp.where(valid, scores, masked_score)
        top = jnp.max(scores, axis=-1, keepdims=True)
        exp_scores = jnp.exp(scores - top)
        total = jnp.sum(exp_scores, axis=-1, keepdims=True)
        added = jnp.dot(exp_scores.astype(BF16), values, preferred_element_type=F32)
        out[i] = (added / total).astype(BF16)


def beta_gamma(place, refs, beta_copies, gamma_copies):
    y, a, h, core = place[1], place[2], place[4], place[5]
    copies = []
    for side in range(2):
        at_core = core if side == 0 else 1 - core
        for i in range(4):
            copies += beta_copies(refs[side * 8 + i], at_core, y ^ i)
        for i in range(4):
            copies += gamma_copies(refs[side * 8 + 4 + i], at_core, h ^ (i >> 1), a ^ (i & 1))
    return copies


def columns(block):
    return pl.ds(pl.multiple_of(block * LANES, LANES), LANES)


def out_kernel(place, att, frames, *refs):
    pieces = refs[0:16]
    mixed, renormed, w, sems = refs[16:]

    def beta(ref, core, y):
        return [
            (ref.at[:, 144 * h : 144 * h + 48, :], w.at[:, h, :, columns(core * 6 + y)]) for h in range(2)
        ]

    def gamma(ref, core, h, a):
        return [(ref.at[:, 0:48, :], w.at[:, h, :, columns(core * 6 + 4 + a)])]

    run_copies(beta_gamma(place, pieces, beta, gamma), sems)()
    total = frames[...].astype(F32)
    for head in range(HEADS):
        mat = w[head].reshape(DH, D)
        total = total + jnp.dot(att[head][:, 0:DH], mat, preferred_element_type=F32)
    total = total.astype(BF16)
    mixed[...] = total
    renormed[...] = norm_rows(total.astype(F32)).astype(BF16)


def glu_kernel(place, length, renormed, *refs):
    pieces_a, pieces_b = refs[0:16], refs[16:24]
    out, w, sems = refs[24:]
    core = place[5]

    def beta(ref, core, y):
        return [
            (ref.at[:, 144 * h + 48 : 144 * h + 144, :], w.at[:, h, :, columns(core * 12 + y)]) for h in range(2)
        ]

    def gamma(ref, core, h, a):
        return [
            (ref.at[:, 48 + 96 * j : 144 + 96 * j, :], w.at[:, h, :, columns(core * 12 + 4 + a * 4 + j)])
            for j in range(2)
        ]

    copies = beta_gamma(place, pieces_a, beta, gamma)
    h, a = place[4], place[2]
    for side in range(2):
        at_core = core if side == 0 else 1 - core
        for i in range(4):
            for j in range(2):
                copies.append(
                    (pieces_b[side * 4 + i].at[:, 96 + 96 * j : 192 + 96 * j, :],
                     w.at[:, h ^ (i >> 1), :, columns(at_core * 12 + 6 + (a ^ (i & 1)) * 4 + j)])
                )
    run_copies(copies, sems)()
    rows = renormed[...]
    first = place[0] * ROWS
    valid = (first + lax.broadcasted_iota(jnp.int32, (ROWS, 1), 0)) < length[0]
    for n in range(6):
        mats = [
            w[:, :, :, at + 256 * n : at + 256 * (n + 1)].reshape(D, 256) for at in (0, D)
        ]
        value, gate = [jnp.dot(rows, mat, preferred_element_type=F32) for mat in mats]
        gated = value * jax.nn.sigmoid(gate)
        out[:, 256 * n : 256 * (n + 1)] = jnp.where(valid, gated, 0.0).astype(BF16)


def conv_kernel(before, gated, after, taps, out, ext, summed):
    ext[0:16, :] = before[...].astype(F32)
    ext[16:144, :] = gated[...].astype(F32)
    ext[144:160, :] = after[...].astype(F32)
    for n in range(D // LANES):
        cols = slice(LANES * n, LANES * (n + 1))
        total = jnp.zeros((ROWS, LANES), F32)
        tap_rows = taps[:, cols].astype(F32)
        for j in range(TAPS):
            total = total + tap_rows[j : j + 1, :] * ext[j + 1 : j + 1 + ROWS, cols]
        summed[:, cols] = total
    for i in range(ROWS // 32):
        rows = slice(32 * i, 32 * (i + 1))
        normed = norm_rows(summed[rows, :])
        out[rows, :] = (normed * jax.nn.sigmoid(normed)).astype(BF16)


def last_kernel(place, activated, mixed, *refs):
    pieces = refs[0:16]
    out, w, sems = refs[16:]

    def beta(ref, core, y):
        return [(ref.at[:, 96 * h : 96 * (h + 1), :], w.at[:, h, :, columns(core * 6 + y)]) for h in range(2)]

    def gamma(ref, core, h, a):
        return [(ref.at[:, 0:96, :], w.at[:, h, :, columns(core * 6 + 4 + a)])]

    run_copies(beta_gamma(place, pieces, beta, gamma), sems)()
    rows = activated[...]
    for n in range(6):
        cols = slice(256 * n, 256 * (n + 1))
        mat = w[:, :, :, cols].reshape(D, 256)
        total = mixed[:, cols].astype(F32) + jnp.dot(rows, mat, preferred_element_type=F32)
        out[:, cols] = total.astype(BF16)


def shape(*dims, dtype=BF16):
    return jax.ShapeDtypeStruct(dims, dtype)


def spread(pack, beta_rows):
    beta, gamma = pack[:, :beta_rows], pack[:, beta_rows:]
    betas = [beta] + [send(beta, xor_y(k)) for k in (1, 2, 3)]
    gammas = [gamma] + [send(gamma, xor_x(k)) for k in (1, 2, 3)]
    own = betas + gammas
    return own + [send(v, SWAP_CORE) for v in own]


def per_device(frames, lengths, w_qkv, w_out, w_glu, depth_kernel, w_conv_out):
    frame_rows = frames[0]
    ctx, fsdp, core = lax.axis_index("ctx"), lax.axis_index("fsdp"), lax.axis_index("dp")
    place = jnp.stack([ctx, ctx % 4, ctx // 4, fsdp // 2, fsdp % 2, core]).astype(jnp.int32)
    hp, gam_a, gam_b = pl.pallas_call(
        pack_kernel,
        out_shape=(shape(528, LANES), shape(240, LANES), shape(288, LANES)),
        in_specs=[SM] + [VM] * 4,
        out_specs=(VM,) * 3,
        compiler_params=params(),
    )(place, w_qkv, w_out, w_glu, w_conv_out)
    hp_other = send(hp, SWAP_H)
    normed = pl.pallas_call(
        norm_kernel, out_shape=shape(ROWS, D), in_specs=[VM], out_specs=VM, compiler_params=params()
    )(frame_rows)
    q_piece, pack_a, pack_b = pl.pallas_call(
        join_kernel,
        out_shape=(shape(2, 288, LANES), shape(528, LANES), shape(480, LANES)),
        in_specs=[SM] + [VM] * 4,
        out_specs=(VM,) * 3,
        compiler_params=params(),
    )(place, hp, hp_other, gam_a, gam_b)
    all_a = lax.all_gather(pack_a, AXES, axis=0, axis_index_groups=Z_GROUPS)
    all_b = lax.all_gather(pack_b, AXES, axis=0, axis_index_groups=Z_GROUPS)

    half = ROWS // 2
    front, back = normed[:half], normed[half:]
    front_other = send(front, SWAP_A)
    backs = [back] + [send(back, shift_y(k)) for k in (1, -1, 2)]
    q_pieces = {0: q_piece}
    for k in (1, 7, 2, 6, 3, 5, 4):
        q_pieces[k] = send(q_piece, shift_z(k))
    back_all = jnp.stack(backs)
    front_both = jnp.stack([front, front_other])
    fronts = [front_both] + [send(front_both, shift_y(k)) for k in (1, -1, 2)]
    back_other = send(back_all, SWAP_A)

    att = pl.pallas_call(
        attend_kernel,
        out_shape=shape(8, ROWS, LANES),
        in_specs=[SM, SM] + [ANY] * 14,
        out_specs=VM,
        scratch_shapes=[
            pltpu.VMEM((8, 2, 64, D), BF16),
            pltpu.VMEM((8, 2, 96, 384), BF16),
            pltpu.VMEM((SEQ, LANES), BF16),
            pltpu.VMEM((SEQ, LANES), BF16),
            pltpu.VMEM((SEQ, LANES), BF16),
            pltpu.SemaphoreType.DMA((40,)),
        ],
        compiler_params=params(),
    )(place, lengths, *fronts, back_all, back_other, *[q_pieces[k] for k in range(8)])
    att = lax.all_to_all(att, "ctx", 0, 0)

    pieces_a = spread(all_a, 288)
    pieces_b = spread(all_b, 192)

    mixed, renormed = pl.pallas_call(
        out_kernel,
        out_shape=(shape(ROWS, D), shape(ROWS, D)),
        in_specs=[SM, VM, VM] + [ANY] * 16,
        out_specs=(VM, VM),
        scratch_shapes=[pltpu.VMEM((8, 2, 48, D), BF16), pltpu.SemaphoreType.DMA((24,))],
        compiler_params=params(),
    )(place, att, frame_rows, *pieces_a)

    gated = pl.pallas_call(
        glu_kernel,
        out_shape=shape(ROWS, D),
        in_specs=[SM, SM, VM] + [ANY] * 24,
        out_specs=VM,
        scratch_shapes=[pltpu.VMEM((8, 2, 96, 2 * D), BF16), pltpu.SemaphoreType.DMA((48,))],
        compiler_params=params(),
    )(place, lengths, renormed, *pieces_a, *pieces_b[4:8], *pieces_b[12:16])

    up = [(i, i + 1) for i in range(7)]
    down = [(i + 1, i) for i in range(7)]
    before = lax.ppermute(gated[ROWS - 16 :], "ctx", up)
    after = lax.ppermute(gated[:16], "ctx", down)
    activated = pl.pallas_call(
        conv_kernel,
        out_shape=shape(ROWS, D),
        in_specs=[VM] * 4,
        out_specs=VM,
        scratch_shapes=[pltpu.VMEM((ROWS + 32, D), F32), pltpu.VMEM((ROWS, D), F32)],
        compiler_params=params(),
    )(before, gated, after, depth_kernel)

    result = pl.pallas_call(
        last_kernel,
        out_shape=shape(ROWS, D),
        in_specs=[SM, VM, VM] + [ANY] * 16,
        out_specs=VM,
        scratch_shapes=[pltpu.VMEM((8, 2, 96, D), BF16), pltpu.SemaphoreType.DMA((24,))],
        compiler_params=params(),
    )(place, activated, mixed, *pieces_b)
    return result[None]


def solution(mesh):
    in_specs = (
        P(("dp", "fsdp"), "ctx", None),
        P(("dp", "fsdp")),
        P("fsdp", None),
        P("fsdp", None),
        P("fsdp", None),
        P(),
        P("fsdp", None),
    )
    out_specs = P(("dp", "fsdp"), "ctx", None)
    return jax.shard_map(
        per_device, mesh=mesh, in_specs=in_specs, out_specs=out_specs, check_vma=False
    )
```

```python
import numpy as np
import jax
import jax.numpy as jnp
from jax import lax
from jax.experimental import pallas as pl
from jax.experimental.pallas import tpu as pltpu
from jax.sharding import PartitionSpec as P

HEADS = 8
DH = 96
TAPS = 31
D = 1536
ROWS = 128
SEQ = 1024
LANES = 128
HALO = 16
WIDE = ROWS + 2 * HALO
masked_score = -1e30

AXES = ("ctx", "fsdp", "dp")
SHAPE = (2, 4, 8, 2, 2)
F32 = jnp.float32
BF16 = jnp.bfloat16


def pairs(move):
    out = []
    for i in range(256):
        c = [int(v) for v in np.unravel_index(i, SHAPE)]
        out.append((i, int(np.ravel_multi_index(move(*c), SHAPE))))
    return out


def xor_y(k):
    return pairs(lambda a, y, z, h, c: (a, y ^ k, z, h, c))


def xor_x(k):
    return pairs(lambda a, y, z, h, c: (a ^ (k & 1), y, z, h ^ (k >> 1), c))


def shift_y(k):
    return pairs(lambda a, y, z, h, c: (a, (y + k) % 4, z, h, c))


def shift_z(k):
    return pairs(lambda a, y, z, h, c: (a, y, (z + k) % 8, h, c))


SWAP_CORE = pairs(lambda a, y, z, h, c: (a, y, z, h, 1 - c))
SWAP_H = pairs(lambda a, y, z, h, c: (a, y, z, 1 - h, c))
SWAP_A = pairs(lambda a, y, z, h, c: (1 - a, y, z, h, c))
Z_GROUPS = [
    [int(np.ravel_multi_index((a, y, z, h, c), SHAPE)) for z in range(8)]
    for a in range(2) for y in range(4) for h in range(2) for c in range(2)
]


def send(value, moves):
    return lax.ppermute(value, AXES, moves)


def params(mib=48):
    return pltpu.CompilerParams(vmem_limit_bytes=mib * 2**20)


VM = pl.BlockSpec(memory_space=pltpu.VMEM)
SM = pl.BlockSpec(memory_space=pltpu.SMEM)
ANY = pl.BlockSpec(memory_space=pl.ANY)


def norm_rows(values):
    middle = jnp.mean(values, axis=-1, keepdims=True)
    apart = values - middle
    spread = jnp.mean(apart * apart, axis=-1, keepdims=True)
    return apart * lax.rsqrt(spread + 1e-05)


def columns(block, count=1):
    return pl.ds(pl.multiple_of(block * LANES, LANES), count * LANES)


def run_copies(copies, sems):
    made = [pltpu.make_async_copy(src, dst, sems.at[i]) for i, (src, dst) in enumerate(copies)]
    for copy in made:
        copy.start()

    def wait():
        for copy in made:
            copy.wait()

    return wait


def pack_kernel(place, w_qkv, w_out, w_glu, w_conv, hp, gam, conv, held, sems):
    ctx, y, a, core = place[0], place[1], place[2], place[5]
    copies = [
        (w_qkv, held),
        (w_out.at[:, columns(core * 6 + y)], hp.at[288:336, :]),
        (w_glu.at[:, columns(core * 12 + y)], hp.at[336:432, :]),
        (w_out.at[:, columns(core * 6 + 4 + a)], gam.at[0:48, :]),
        (w_conv.at[:, columns(core * 6, 6)], conv),
    ]
    for j in range(4):
        copies.append((w_glu.at[:, columns(core * 12 + 4 + a * 4 + j)], gam.at[48 + 96 * j : 144 + 96 * j, :]))
    wait = run_copies(copies, sems)
    hp[0:288, :] = jnp.zeros((288, LANES), BF16)
    wait()
    for j in range(HEADS):

        @pl.when(ctx == j)
        def _():
            for part in range(3):
                first = part * 768 + DH * j
                hp[96 * part : 96 * (part + 1), 0:DH] = held[:, first : first + DH]


def join_kernel(place, own, other, gam, pack, sems):
    h = place[4]
    copies = [(gam, pack.at[864:1296, :])]
    for ref, at in ((own, h), (other, 1 - h)):
        copies.append((ref.at[0:288, :], pack.at[pl.ds(pl.multiple_of(at * 288, 32), 288), :]))
        copies.append((ref.at[288:432, :], pack.at[pl.ds(pl.multiple_of(576 + at * 144, 16), 144), :]))
    run_copies(copies, sems)()


def stack_kernel(place, own, other, both, sems):
    h = place[4]
    run_copies([(own, both.at[h]), (other, both.at[1 - h])], sems)()


def norm_kernel(x, out):
    out[...] = norm_rows(x[...].astype(F32)).astype(BF16)


def attend_kernel(place, length, *refs):
    front, back, weights = refs[0:4], refs[4:6], refs[6]
    out, x, w, q, k, v, att, sems = refs[7:]
    y, a = place[1], place[2]
    copies = []
    for part in range(3):
        for h in range(2):
            first = 288 * h + 96 * part
            copies.append(
                (weights.at[:, first : first + 96, :], w.at[:, h, :, LANES * part : LANES * (part + 1)])
            )
    for i, step in enumerate((0, -1, 1, -2)):
        at = (y + step + 4) % 4
        for side in range(2):
            there = a if side == 0 else 1 - a
            copies.append((front[i].at[side], x.at[there * 4 + at, 0]))
            copies.append((back[side].at[i], x.at[there * 4 + at, 1]))
    wait = run_copies(copies, sems)
    att[0:HALO, :] = jnp.zeros((HALO, LANES), BF16)
    att[SEQ + HALO : SEQ + 2 * HALO, :] = jnp.zeros((HALO, LANES), BF16)
    wait()
    mat = w[...].reshape(D, 3 * LANES)
    for i in range(4):
        rows = slice(256 * i, 256 * (i + 1))
        made = jnp.dot(x[2 * i : 2 * i + 2].reshape(256, D), mat, preferred_element_type=F32).astype(BF16)
        for part, ref in enumerate((q, k, v)):
            ref[rows, :] = made[:, LANES * part : LANES * (part + 1)]
    valid = lax.broadcasted_iota(jnp.int32, (1, SEQ), 1) < length[0]
    keys, values = k[...], v[...]
    for i in range(HEADS):
        scores = lax.dot_general(
            q[ROWS * i : ROWS * (i + 1), :], keys, (((1,), (1,)), ((), ())), preferred_element_type=F32
        )
        scores = jnp.where(valid, scores, masked_score)
        top = jnp.max(scores, axis=-1, keepdims=True)
        exp_scores = jnp.exp((scores - top) * DH ** (-0.5))
        total = jnp.sum(exp_scores, axis=-1, keepdims=True)
        added = jnp.dot(exp_scores.astype(BF16), values, preferred_element_type=F32)
        att[HALO + ROWS * i : HALO + ROWS * (i + 1), :] = (added / total).astype(BF16)
    for i in range(HEADS):
        out[i] = att[ROWS * i : ROWS * i + WIDE, :]


def beta_gamma(place, refs, beta_copies, gamma_copies):
    y, a, h, core = place[1], place[2], place[4], place[5]
    copies = []
    for side in range(2):
        at_core = core if side == 0 else 1 - core
        for i in range(4):
            copies += beta_copies(refs[side * 8 + i], at_core, y ^ i)
        for i in range(4):
            copies += gamma_copies(refs[side * 8 + 4 + i], at_core, h ^ (i >> 1), a ^ (i & 1))
    return copies


def out_kernel(place, att, frames, before, after, *refs):
    pieces = refs[0:16]
    mixed, renormed, w, sems = refs[16:]

    def beta(ref, core, y):
        return [
            (ref.at[:, 144 * h : 144 * h + 48, :], w.at[:, h, :, columns(core * 6 + y)]) for h in range(2)
        ]

    def gamma(ref, core, h, a):
        return [(ref.at[:, 0:48, :], w.at[:, h, :, columns(core * 6 + 4 + a)])]

    run_copies(beta_gamma(place, pieces, beta, gamma), sems)()
    total = jnp.concatenate([before[...], frames[...], after[...]], axis=0).astype(F32)
    for head in range(HEADS):
        mat = w[head].reshape(DH, D)
        total = total + jnp.dot(att[head][:, 0:DH], mat, preferred_element_type=F32)
    total = total.astype(BF16)
    mixed[...] = total[HALO : HALO + ROWS]
    renormed[...] = norm_rows(total.astype(F32)).astype(BF16)


def glu_kernel(place, length, renormed, *refs):
    pieces = refs[0:16]
    out, w, sems = refs[16:]

    def beta(ref, core, y):
        return [
            (ref.at[:, 144 * h + 48 : 144 * h + 144, :], w.at[:, h, :, columns(core * 12 + y)]) for h in range(2)
        ]

    def gamma(ref, core, h, a):
        return [
            (ref.at[:, 48 + 96 * j : 144 + 96 * j, :], w.at[:, h, :, columns(core * 12 + 4 + a * 4 + j)])
            for j in range(4)
        ]

    run_copies(beta_gamma(place, pieces, beta, gamma), sems)()
    rows = renormed[...]
    position = place[0] * ROWS - HALO + lax.broadcasted_iota(jnp.int32, (WIDE, 1), 0)
    valid = (position >= 0) & (position < length[0])
    for n in range(6):
        mats = [
            w[:, :, :, at + 256 * n : at + 256 * (n + 1)].reshape(D, 256) for at in (0, D)
        ]
        value, gate = [jnp.dot(rows, mat, preferred_element_type=F32) for mat in mats]
        gated = value * jax.nn.sigmoid(gate)
        out[:, 256 * n : 256 * (n + 1)] = jnp.where(valid, gated, 0.0).astype(BF16)


def conv_kernel(gated, taps, out, ext, summed):
    ext[...] = gated[...].astype(F32)
    for n in range(D // LANES):
        cols = slice(LANES * n, LANES * (n + 1))
        total = jnp.zeros((ROWS, LANES), F32)
        tap_rows = taps[:, cols].astype(F32)
        for j in range(TAPS):
            total = total + tap_rows[j : j + 1, :] * ext[j + 1 : j + 1 + ROWS, cols]
        summed[:, cols] = total
    for i in range(ROWS // 32):
        rows = slice(32 * i, 32 * (i + 1))
        normed = norm_rows(summed[rows, :])
        out[rows, :] = (normed * jax.nn.sigmoid(normed)).astype(BF16)


def last_kernel(place, activated, mixed, *refs):
    pieces = refs[0:2]
    out, w, sems = refs[2:]
    core = place[5]
    copies = [(piece, w.at[at]) for piece, at in zip(pieces, (core, 1 - core))]
    run_copies(copies, sems)()
    rows = activated[...]
    for n in range(6):
        cols = slice(256 * n, 256 * (n + 1))
        mat = w[n // 3, :, :, :, 256 * (n % 3) : 256 * (n % 3 + 1)].reshape(D, 256)
        total = mixed[:, cols].astype(F32) + jnp.dot(rows, mat, preferred_element_type=F32)
        out[:, cols] = total.astype(BF16)


def shape(*dims, dtype=BF16):
    return jax.ShapeDtypeStruct(dims, dtype)


def spread(beta, gamma):
    betas = [beta] + [send(beta, xor_y(k)) for k in (1, 2, 3)]
    gammas = [gamma] + [send(gamma, xor_x(k)) for k in (1, 2, 3)]
    own = betas + gammas
    return own + [send(v, SWAP_CORE) for v in own]


def per_device(frames, lengths, w_qkv, w_out, w_glu, depth_kernel, w_conv_out):
    frame_rows = frames[0]
    ctx, fsdp, core = lax.axis_index("ctx"), lax.axis_index("fsdp"), lax.axis_index("dp")
    place = jnp.stack([ctx, ctx & 3, ctx >> 2, fsdp >> 1, fsdp & 1, core]).astype(jnp.int32)
    hp, gam, conv = pl.pallas_call(
        pack_kernel,
        out_shape=(shape(432, LANES), shape(432, LANES), shape(96, 768)),
        in_specs=[SM] + [ANY] * 4,
        out_specs=(VM,) * 3,
        scratch_shapes=[pltpu.VMEM((96, 2304), BF16), pltpu.SemaphoreType.DMA((9,))],
        compiler_params=params(),
    )(place, w_qkv, w_out, w_glu, w_conv_out)
    hp_other = send(hp, SWAP_H)
    normed = pl.pallas_call(
        norm_kernel, out_shape=shape(ROWS, D), in_specs=[VM], out_specs=VM, compiler_params=params()
    )(frame_rows)
    pack = pl.pallas_call(
        join_kernel,
        out_shape=shape(1296, LANES),
        in_specs=[SM] + [VM] * 3,
        out_specs=VM,
        scratch_shapes=[pltpu.SemaphoreType.DMA((5,))],
        compiler_params=params(),
    )(place, hp, hp_other, gam)
    gathered = lax.all_gather(pack, AXES, axis=0, axis_index_groups=Z_GROUPS)

    half = ROWS // 2
    front, back = normed[:half], normed[half:]
    front_other = send(front, SWAP_A)
    backs = [back] + [send(back, shift_y(k)) for k in (1, -1, 2)]
    back_all = jnp.stack(backs)
    front_both = jnp.stack([front, front_other])
    fronts = [front_both] + [send(front_both, shift_y(k)) for k in (1, -1, 2)]
    back_other = send(back_all, SWAP_A)
    conv_other = send(conv, SWAP_H)
    up = [(i, i + 1) for i in range(7)]
    down = [(i + 1, i) for i in range(7)]
    before = lax.ppermute(frame_rows[ROWS - HALO :], "ctx", up)
    after = lax.ppermute(frame_rows[:HALO], "ctx", down)
    conv_both = pl.pallas_call(
        stack_kernel,
        out_shape=shape(2, 96, 768),
        in_specs=[SM] + [VM] * 2,
        out_specs=VM,
        scratch_shapes=[pltpu.SemaphoreType.DMA((2,))],
        compiler_params=params(),
    )(place, conv, conv_other)

    pieces = spread(gathered[:, 576:864], gathered[:, 864:])
    gathered_conv = lax.all_gather(conv_both, AXES, axis=0, axis_index_groups=Z_GROUPS)
    conv_pieces = [gathered_conv, send(gathered_conv, SWAP_CORE)]

    att = pl.pallas_call(
        attend_kernel,
        out_shape=shape(8, WIDE, LANES),
        in_specs=[SM, SM] + [ANY] * 7,
        out_specs=VM,
        scratch_shapes=[
            pltpu.VMEM((8, 2, 64, D), BF16),
            pltpu.VMEM((8, 2, 96, 384), BF16),
            pltpu.VMEM((SEQ, LANES), BF16),
            pltpu.VMEM((SEQ, LANES), BF16),
            pltpu.VMEM((SEQ, LANES), BF16),
            pltpu.VMEM((SEQ + 2 * HALO, LANES), BF16),
            pltpu.SemaphoreType.DMA((22,)),
        ],
        compiler_params=params(),
    )(place, lengths, *fronts, back_all, back_other, gathered)
    att = lax.all_to_all(att, "ctx", 0, 0)

    mixed, renormed = pl.pallas_call(
        out_kernel,
        out_shape=(shape(ROWS, D), shape(WIDE, D)),
        in_specs=[SM] + [VM] * 4 + [ANY] * 16,
        out_specs=(VM, VM),
        scratch_shapes=[pltpu.VMEM((8, 2, 48, D), BF16), pltpu.SemaphoreType.DMA((24,))],
        compiler_params=params(),
    )(place, att, frame_rows, before, after, *pieces)

    gated = pl.pallas_call(
        glu_kernel,
        out_shape=shape(WIDE, D),
        in_specs=[SM, SM, VM] + [ANY] * 16,
        out_specs=VM,
        scratch_shapes=[pltpu.VMEM((8, 2, 96, 2 * D), BF16), pltpu.SemaphoreType.DMA((48,))],
        compiler_params=params(),
    )(place, lengths, renormed, *pieces)

    activated = pl.pallas_call(
        conv_kernel,
        out_shape=shape(ROWS, D),
        in_specs=[VM] * 2,
        out_specs=VM,
        scratch_shapes=[pltpu.VMEM((WIDE, D), F32), pltpu.VMEM((ROWS, D), F32)],
        compiler_params=params(),
    )(gated, depth_kernel)

    result = pl.pallas_call(
        last_kernel,
        out_shape=shape(ROWS, D),
        in_specs=[SM, VM, VM] + [ANY] * 2,
        out_specs=VM,
        scratch_shapes=[pltpu.VMEM((2, 8, 2, 96, 768), BF16), pltpu.SemaphoreType.DMA((2,))],
        compiler_params=params(),
    )(place, activated, mixed, *conv_pieces)
    return result[None]


def solution(mesh):
    in_specs = (
        P(("dp", "fsdp"), "ctx", None),
        P(("dp", "fsdp")),
        P("fsdp", None),
        P("fsdp", None),
        P("fsdp", None),
        P(),
        P("fsdp", None),
    )
    out_specs = P(("dp", "fsdp"), "ctx", None)
    return jax.shard_map(
        per_device, mesh=mesh, in_specs=in_specs, out_specs=out_specs, check_vma=False
    )
```

```python
import numpy as np
import jax
import jax.numpy as jnp
from jax import lax
from jax.experimental import pallas as pl
from jax.experimental.pallas import tpu as pltpu
from jax.sharding import PartitionSpec as P

HEADS = 8
DH = 96
TAPS = 31
D = 1536
ROWS = 128
SEQ = 1024
LANES = 128
HALO = 16
WIDE = ROWS + 2 * HALO
masked_score = -1e30

AXES = ("ctx", "fsdp", "dp")
SHAPE = (2, 4, 8, 2, 2)
F32 = jnp.float32
BF16 = jnp.bfloat16


def pairs(move):
    out = []
    for i in range(256):
        c = [int(v) for v in np.unravel_index(i, SHAPE)]
        out.append((i, int(np.ravel_multi_index(move(*c), SHAPE))))
    return out


def xor_y(k):
    return pairs(lambda a, y, z, h, c: (a, y ^ k, z, h, c))


def xor_x(k):
    return pairs(lambda a, y, z, h, c: (a ^ (k & 1), y, z, h ^ (k >> 1), c))


def shift_z(k):
    return pairs(lambda a, y, z, h, c: (a, y, (z + k) % 8, h, c))


SWAP_CORE = pairs(lambda a, y, z, h, c: (a, y, z, h, 1 - c))
SWAP_H = pairs(lambda a, y, z, h, c: (a, y, z, 1 - h, c))

def send(value, moves):
    return lax.ppermute(value, AXES, moves)


def params(mib=60):
    return pltpu.CompilerParams(vmem_limit_bytes=mib * 2**20)


def cost(flops):
    return pl.CostEstimate(flops=flops, bytes_accessed=2**20, transcendentals=0)


def after(value, *others):
    return lax.optimization_barrier((value,) + others)[0]


def whereabouts():
    ctx, fsdp = lax.axis_index("ctx"), lax.axis_index("fsdp")
    return ctx, ctx & 3, ctx >> 2, fsdp >> 1, fsdp & 1, lax.axis_index("dp")


VM = pl.BlockSpec(memory_space=pltpu.VMEM)
SM = pl.BlockSpec(memory_space=pltpu.SMEM)
ANY = pl.BlockSpec(memory_space=pl.ANY)


def norm_rows(values):
    middle = jnp.mean(values, axis=-1, keepdims=True)
    apart = values - middle
    spread = jnp.mean(apart * apart, axis=-1, keepdims=True)
    return apart * lax.rsqrt(spread + 1e-05)


def columns(block, count=1):
    return pl.ds(pl.multiple_of(block * LANES, LANES), count * LANES)


def run_copies(copies, sems):
    made = [pltpu.make_async_copy(src, dst, sems.at[i]) for i, (src, dst) in enumerate(copies)]
    for copy in made:
        copy.start()

    def wait():
        for copy in made:
            copy.wait()

    return wait


BETA, GAMMA = 480, 528
NEAR = BETA // 2 + 288


def pack_kernel(x, w_qkv, w_out, w_glu, w_conv, beta, gam, normed, held, rows, sems):
    ctx, y, a, _, _, core = whereabouts()
    glu, conv = core * 12, core * 6
    copies = [
        (w_qkv, held),
        (x, rows),
        (w_out.at[:, columns(conv + y)], beta.at[0:48, :]),
        (w_glu.at[:, columns(glu + y)], beta.at[48:144, :]),
        (w_glu.at[0:48, columns(glu + 4 + y)], beta.at[144:192, :]),
        (w_conv.at[0:48, columns(conv + y)], beta.at[192:240, :]),
        (w_out.at[:, columns(conv + 4 + a)], gam.at[0:48, :]),
        (w_conv.at[:, columns(conv + 4 + a)], gam.at[432:528, :]),
    ]
    for j in range(2):
        copies.append((w_glu.at[48:96, columns(glu + 4 + 2 * a + j)], gam.at[48 + 48 * j : 96 + 48 * j, :]))
        copies.append((w_glu.at[:, columns(glu + 8 + 2 * a + j)], gam.at[144 + 96 * j : 240 + 96 * j, :]))
        copies.append((w_conv.at[48:96, columns(conv + 2 * a + j)], gam.at[336 + 48 * j : 384 + 48 * j, :]))
    wait = run_copies(copies, sems)
    beta[240:528, :] = jnp.zeros((288, LANES), BF16)
    wait()
    for j in range(HEADS):

        @pl.when(ctx == j)
        def _():
            for part in range(3):
                first = part * 768 + DH * j
                beta[240 + 96 * part : 336 + 96 * part, 0:DH] = held[:, first : first + DH]

    normed[...] = norm_rows(rows[...].astype(F32)).astype(BF16)


STEPS = (0, -1, -2, -3, 1, 2, 3)


def order_kernel(*refs):
    blocks, low, high, w, beta, gam = refs[0:7], refs[7], refs[8], refs[9], refs[10], refs[11]
    _, _, _, z, _, _ = whereabouts()

    def near(ref, at):
        for side in range(2):
            first = NEAR * side
            beta[at, 240 * side : 240 * (side + 1), :] = ref[first : first + 240, :]
            for part in range(3):
                start = first + 240 + 96 * part
                w[at, side, :, LANES * part : LANES * (part + 1)] = ref[start : start + 96, :]

    near(low, z ^ 4)
    gam[z ^ 4] = high[...]
    for ref, step in zip(blocks, STEPS):
        at = (z + step) & 7
        near(ref, at)
        gam[at] = ref[2 * NEAR :, :]


def attend_kernel(length, x, w, out, q, k, v, att):
    att[0:HALO, :] = jnp.zeros((HALO, LANES), BF16)
    att[SEQ + HALO : SEQ + 2 * HALO, :] = jnp.zeros((HALO, LANES), BF16)
    mat = w[...].reshape(D, 3 * LANES)
    for i in range(4):
        rows = slice(256 * i, 256 * (i + 1))
        made = jnp.dot(x[2 * i : 2 * i + 2].reshape(256, D), mat, preferred_element_type=F32).astype(BF16)
        for part, ref in enumerate((q, k, v)):
            ref[rows, :] = made[:, LANES * part : LANES * (part + 1)]
    valid = lax.broadcasted_iota(jnp.int32, (1, SEQ), 1) < length[0]
    keys, values = k[...], v[...]
    for i in range(HEADS):
        scores = lax.dot_general(
            q[ROWS * i : ROWS * (i + 1), :], keys, (((1,), (1,)), ((), ())), preferred_element_type=F32
        )
        scores = jnp.where(valid, scores, masked_score)
        top = jnp.max(scores, axis=-1, keepdims=True)
        exp_scores = jnp.exp((scores - top) * DH ** (-0.5))
        total = jnp.sum(exp_scores, axis=-1, keepdims=True)
        added = jnp.dot(exp_scores.astype(BF16), values, preferred_element_type=F32)
        att[HALO + ROWS * i : HALO + ROWS * (i + 1), :] = (added / total).astype(BF16)
    for i in range(HEADS):
        out[i] = att[ROWS * i : ROWS * i + WIDE, :]


def cut_kernel(beta_1, beta_3, gamma_1, gamma_3, beta_low, beta_high, gamma_low, gamma_high, sems):
    run_copies(
        [
            (beta_1.at[0:4], beta_low), (beta_3.at[4:8], beta_high),
            (gamma_1.at[0:4], gamma_low), (gamma_3.at[4:8], gamma_high),
        ],
        sems,
    )()


def halves(refs):
    whole, low, high = slice(0, 8), slice(0, 4), slice(4, 8)
    return list(zip((0, 1, 2, 2, 3), (whole, whole, low, high, whole), refs))


def middle_kernel(length, att_in, frames_in, before_in, behind_in, taps_in, *refs):
    pieces = refs[0:20]
    out, att, frames, taps, w_out, w, w_conv, ext, summed, own_sems, out_sems, glu_sems, conv_sems = refs[20:]
    own_wait = run_copies(
        [
            (att_in, att), (before_in, frames.at[0:HALO]), (frames_in, frames.at[HALO : HALO + ROWS]),
            (behind_in, frames.at[HALO + ROWS :]), (taps_in, taps),
        ],
        own_sems,
    )
    _, y, a, _, h, core = whereabouts()
    owners = [(0, core), (10, 1 - core)]

    def glu_copy(source, z, rows, h, block):
        target = w.at[z, h, rows, columns(block)]
        pltpu.make_async_copy(source, target, glu_sems.at[block]).start()

    def conv_copy(source, z, rows, h, block):
        target = w_conv.at[z, h, rows, columns(block)]
        pltpu.make_async_copy(source, target, conv_sems.at[0]).start()

    def glu_wait(block):
        target = w.at[:, :, :, LANES * block : LANES * (block + 1)]
        pltpu.make_async_copy(target, target, glu_sems.at[block]).wait()

    copies = []
    for first, at in owners:
        for i, z, ref in halves(pieces[first : first + 5]):
            for side in range(2):
                start = 240 * side
                copies.append((ref.at[:, start : start + 48, :], w_out.at[z, side, :, columns(at * 6 + (y ^ i))]))
        for i, z, ref in halves(pieces[first + 5 : first + 10]):
            copies.append((ref.at[:, 0:48, :], w_out.at[z, h ^ (i >> 1), :, columns(at * 6 + 4 + (a ^ (i & 1)))]))
    out_wait = run_copies(copies, out_sems)
    whole, low, high = slice(0, 96), slice(0, 48), slice(48, 96)
    for first, at in owners:
        for i, z, ref in halves(pieces[first : first + 5]):
            for side in range(2):
                start = 240 * side + 48
                glu_copy(ref.at[:, start : start + 96, :], z, whole, side, at * 12 + (y ^ i))
    for first, at in owners:
        for i, z, ref in halves(pieces[first : first + 5]):
            for side in range(2):
                start = 240 * side + 144
                glu_copy(ref.at[:, start : start + 48, :], z, low, side, at * 12 + 4 + (y ^ i))
        for i, z, ref in halves(pieces[first + 5 : first + 10]):
            block = at * 12 + 4 + 2 * (a ^ (i & 1))
            for j in range(2):
                start = 48 + 48 * j
                glu_copy(ref.at[:, start : start + 48, :], z, high, h ^ (i >> 1), block + j)
    for first, at in owners:
        for i, z, ref in halves(pieces[first + 5 : first + 10]):
            block = at * 12 + 8 + 2 * (a ^ (i & 1))
            for j in range(2):
                start = 144 + 96 * j
                glu_copy(ref.at[:, start : start + 96, :], z, whole, h ^ (i >> 1), block + j)

    for first, at in owners:
        for i, z, ref in halves(pieces[first : first + 5]):
            for side in range(2):
                start = 240 * side + 192
                conv_copy(ref.at[:, start : start + 48, :], z, low, side, at * 6 + (y ^ i))
        for i, z, ref in halves(pieces[first + 5 : first + 10]):
            there = a ^ (i & 1)
            for j in range(2):
                start = 336 + 48 * j
                conv_copy(ref.at[:, start : start + 48, :], z, high, h ^ (i >> 1), at * 6 + 2 * there + j)
            conv_copy(ref.at[:, 432:528, :], z, whole, h ^ (i >> 1), at * 6 + 4 + there)

    out_wait()
    own_wait()
    total = frames[...].astype(F32)
    for head in range(HEADS):
        mat = w_out[head].reshape(DH, D)
        total = total + jnp.dot(att[head][:, 0:DH], mat, preferred_element_type=F32)
    total = total.astype(BF16)
    mixed = total[HALO : HALO + ROWS]
    rows = norm_rows(total.astype(F32)).astype(BF16)

    position = lax.axis_index("ctx") * ROWS - HALO + lax.broadcasted_iota(jnp.int32, (WIDE, 1), 0)
    valid = (position >= 0) & (position < length[0])
    for n in range(6):
        for block in (2 * n, 2 * n + 1, 12 + 2 * n, 13 + 2 * n):
            glu_wait(block)
        mats = [
            w[:, :, :, at + 256 * n : at + 256 * (n + 1)].reshape(D, 256) for at in (0, D)
        ]
        value, gate = [jnp.dot(rows, mat, preferred_element_type=F32) for mat in mats]
        gated = value * jax.nn.sigmoid(gate)
        ext[:, 256 * n : 256 * (n + 1)] = jnp.where(valid, gated, 0.0).astype(BF16).astype(F32)
        for m in (2 * n, 2 * n + 1):
            cols = slice(LANES * m, LANES * (m + 1))
            total = jnp.zeros((ROWS, LANES), F32)
            tap_rows = taps[:, cols].astype(F32)
            for j in range(TAPS):
                total = total + tap_rows[j : j + 1, :] * ext[j + 1 : j + 1 + ROWS, cols]
            summed[:, cols] = total
    normed = norm_rows(summed[...])
    activated = (normed * jax.nn.sigmoid(normed)).astype(BF16)
    pltpu.make_async_copy(w_conv, w_conv, conv_sems.at[0]).wait()
    for n in range(6):
        cols = slice(256 * n, 256 * (n + 1))
        mat = w_conv[:, :, :, cols].reshape(D, 256)
        total = mixed[:, cols].astype(F32) + jnp.dot(activated, mat, preferred_element_type=F32)
        out[:, cols] = total.astype(BF16)


def shape(*dims, dtype=BF16):
    return jax.ShapeDtypeStruct(dims, dtype)


def ring_z(own, low, high):
    below, above = [own], [own]
    for _ in range(3):
        below.append(send(below[-1], shift_z(1)))
        above.append(send(above[-1], shift_z(-1)))
    return below + above[1:] + [send(low(below[3]), shift_z(1)), send(high(above[3]), shift_z(-1))]


def per_device(frames, lengths, w_qkv, w_out, w_glu, depth_kernel, w_conv_out):
    frame_rows = frames[0]
    near, gamma, normed = pl.pallas_call(
        pack_kernel,
        out_shape=(shape(NEAR, LANES), shape(GAMMA, LANES), shape(ROWS, D)),
        in_specs=[ANY] * 5,
        out_specs=(VM,) * 3,
        scratch_shapes=[
            pltpu.VMEM((96, 2304), BF16), pltpu.VMEM((ROWS, D), BF16), pltpu.SemaphoreType.DMA((14,))
        ],
        compiler_params=params(),
    )(frame_rows, w_qkv, w_out, w_glu, w_conv_out)
    far = send(near, SWAP_H)
    every = lax.all_to_all(jnp.broadcast_to(normed[None], (8, ROWS, D)), "ctx", 0, 0)

    _, _, _, _, h, _ = whereabouts()
    pack = jnp.concatenate([jnp.where(h == 0, near, far), jnp.where(h == 0, far, near), gamma], axis=0)
    blocks = ring_z(pack, lambda v: v[: 2 * NEAR], lambda v: v[2 * NEAR :])
    w_head, beta, gamma = pl.pallas_call(
        order_kernel,
        out_shape=(shape(8, 2, 96, 3 * LANES), shape(8, BETA, LANES), shape(8, GAMMA, LANES)),
        in_specs=[VM] * 9,
        out_specs=(VM,) * 3,
        compiler_params=params(16),
    )(*blocks)

    gamma_1, gamma_3 = send(gamma, xor_x(1)), send(gamma, xor_x(3))
    beta_1, beta_3 = send(beta, xor_y(1)), send(beta, xor_y(3))
    beta_other, gamma_other = send(beta, SWAP_CORE), send(gamma, SWAP_CORE)

    att = pl.pallas_call(
        attend_kernel,
        out_shape=shape(8, WIDE, LANES),
        in_specs=[SM, VM, VM],
        out_specs=VM,
        scratch_shapes=[
            pltpu.VMEM((SEQ, LANES), BF16),
            pltpu.VMEM((SEQ, LANES), BF16),
            pltpu.VMEM((SEQ, LANES), BF16),
            pltpu.VMEM((SEQ + 2 * HALO, LANES), BF16),
        ],
        cost_estimate=cost(2 * 10**10),
        compiler_params=params(16),
    )(lengths, every, after(w_head, beta_other, gamma_other))

    up = [(i, i + 1) for i in range(7)]
    down = [(i + 1, i) for i in range(7)]
    halo = after(frame_rows, att)
    att = lax.all_to_all(att, "ctx", 0, 0)
    frames_before = lax.ppermute(halo[ROWS - HALO :], "ctx", up)
    frames_behind = lax.ppermute(halo[:HALO], "ctx", down)
    beta_1, beta_3, gamma_1, gamma_3, att, frames_before, frames_behind = lax.optimization_barrier(
        (beta_1, beta_3, gamma_1, gamma_3, att, frames_before, frames_behind)
    )
    beta_2, beta_2b, gamma_2, gamma_2b = pl.pallas_call(
        cut_kernel,
        out_shape=(shape(4, BETA, LANES),) * 2 + (shape(4, GAMMA, LANES),) * 2,
        in_specs=[ANY] * 4,
        out_specs=(VM,) * 4,
        scratch_shapes=[pltpu.SemaphoreType.DMA((4,))],
        compiler_params=params(16),
    )(beta_1, beta_3, gamma_1, gamma_3)
    beta_2, beta_2b = send(beta_2, xor_y(3)), send(beta_2b, xor_y(1))
    gamma_2, gamma_2b = send(gamma_2, xor_x(3)), send(gamma_2b, xor_x(1))
    swapped_1 = [send(v, SWAP_CORE) for v in (beta_1, beta_3, gamma_1, gamma_3)]
    second = [beta_2, beta_2b, gamma_2, gamma_2b]
    swapped_2 = [send(v, SWAP_CORE) for v in second]
    pieces = [
        beta, beta_1, beta_2, beta_2b, beta_3, gamma, gamma_1, gamma_2, gamma_2b, gamma_3,
        beta_other, swapped_1[0], swapped_2[0], swapped_2[1], swapped_1[1],
        gamma_other, swapped_1[2], swapped_2[2], swapped_2[3], swapped_1[3],
    ]

    result = pl.pallas_call(
        middle_kernel,
        out_shape=shape(ROWS, D),
        in_specs=[SM] + [ANY] * 25,
        out_specs=VM,
        scratch_shapes=[
            pltpu.VMEM((8, WIDE, LANES), BF16),
            pltpu.VMEM((WIDE, D), BF16),
            pltpu.VMEM((TAPS, D), BF16),
            pltpu.VMEM((8, 2, 48, D), BF16),
            pltpu.VMEM((8, 2, 96, 2 * D), BF16),
            pltpu.VMEM((8, 2, 96, D), BF16),
            pltpu.VMEM((WIDE, D), F32),
            pltpu.VMEM((ROWS, D), F32),
            pltpu.SemaphoreType.DMA((5,)),
            pltpu.SemaphoreType.DMA((30,)),
            pltpu.SemaphoreType.DMA((24,)),
            pltpu.SemaphoreType.DMA((1,)),
        ],
        compiler_params=params(26),
    )(lengths, att, frame_rows, frames_before, frames_behind, depth_kernel, *pieces)
    return result[None]


def solution(mesh):
    in_specs = (
        P(("dp", "fsdp"), "ctx", None),
        P(("dp", "fsdp")),
        P("fsdp", None),
        P("fsdp", None),
        P("fsdp", None),
        P(),
        P("fsdp", None),
    )
    out_specs = P(("dp", "fsdp"), "ctx", None)
    return jax.shard_map(
        per_device, mesh=mesh, in_specs=in_specs, out_specs=out_specs, check_vma=False
    )
```

```python
import numpy as np
import jax
import jax.numpy as jnp
from jax import lax
from jax.experimental import pallas as pl
from jax.experimental.pallas import tpu as pltpu
from jax.sharding import PartitionSpec as P

HEADS = 8
DH = 96
TAPS = 31
D = 1536
ROWS = 128
SEQ = 1024
LANES = 128
HALO = 16
WIDE = ROWS + 2 * HALO
masked_score = -1e30

AXES = ("ctx", "fsdp", "dp")
SHAPE = (2, 4, 8, 2, 2)
F32 = jnp.float32
BF16 = jnp.bfloat16


def pairs(move):
    out = []
    for i in range(256):
        c = [int(v) for v in np.unravel_index(i, SHAPE)]
        out.append((i, int(np.ravel_multi_index(move(*c), SHAPE))))
    return out


def xor_y(k):
    return pairs(lambda a, y, z, h, c: (a, y ^ k, z, h, c))


def xor_x(k):
    return pairs(lambda a, y, z, h, c: (a ^ (k & 1), y, z, h ^ (k >> 1), c))


def shift_z(k):
    return pairs(lambda a, y, z, h, c: (a, y, (z + k) % 8, h, c))


SWAP_CORE = pairs(lambda a, y, z, h, c: (a, y, z, h, 1 - c))
SWAP_H = pairs(lambda a, y, z, h, c: (a, y, z, 1 - h, c))

def send(value, moves):
    return lax.ppermute(value, AXES, moves)


def params(mib=60):
    return pltpu.CompilerParams(vmem_limit_bytes=mib * 2**20)


def cost(flops):
    return pl.CostEstimate(flops=flops, bytes_accessed=2**20, transcendentals=0)


def after(value, *others):
    return lax.optimization_barrier((value,) + others)[0]


def whereabouts():
    ctx, fsdp = lax.axis_index("ctx"), lax.axis_index("fsdp")
    return ctx, ctx & 3, ctx >> 2, fsdp >> 1, fsdp & 1, lax.axis_index("dp")


VM = pl.BlockSpec(memory_space=pltpu.VMEM)
SM = pl.BlockSpec(memory_space=pltpu.SMEM)
ANY = pl.BlockSpec(memory_space=pl.ANY)


def norm_rows(values):
    middle = jnp.mean(values, axis=-1, keepdims=True)
    apart = values - middle
    spread = jnp.mean(apart * apart, axis=-1, keepdims=True)
    return apart * lax.rsqrt(spread + 1e-05)


def columns(block, count=1):
    return pl.ds(pl.multiple_of(block * LANES, LANES), count * LANES)


def run_copies(copies, sems):
    made = [pltpu.make_async_copy(src, dst, sems.at[i]) for i, (src, dst) in enumerate(copies)]
    for copy in made:
        copy.start()

    def wait():
        for copy in made:
            copy.wait()

    return wait


BETA, GAMMA = 480, 528
NEAR = BETA // 2 + 224


def pack_kernel(x, w_qkv, w_out, w_glu, w_conv, beta, gam, normed, held, head, rows, sems):
    ctx, y, a, _, _, core = whereabouts()
    glu, conv = core * 12, core * 6
    copies = [
        (w_qkv, held),
        (x, rows),
        (w_out.at[:, columns(conv + y)], beta.at[0:48, :]),
        (w_glu.at[:, columns(glu + y)], beta.at[48:144, :]),
        (w_glu.at[0:48, columns(glu + 4 + y)], beta.at[144:192, :]),
        (w_conv.at[0:48, columns(conv + y)], beta.at[192:240, :]),
        (w_out.at[:, columns(conv + 4 + a)], gam.at[0:48, :]),
        (w_conv.at[:, columns(conv + 4 + a)], gam.at[432:528, :]),
    ]
    for j in range(2):
        copies.append((w_glu.at[48:96, columns(glu + 4 + 2 * a + j)], gam.at[48 + 48 * j : 96 + 48 * j, :]))
        copies.append((w_glu.at[:, columns(glu + 8 + 2 * a + j)], gam.at[144 + 96 * j : 240 + 96 * j, :]))
        copies.append((w_conv.at[48:96, columns(conv + 2 * a + j)], gam.at[336 + 48 * j : 384 + 48 * j, :]))
    wait = run_copies(copies, sems)
    beta[432:464, :] = jnp.zeros((32, LANES), BF16)
    wait()
    for j in range(HEADS):

        @pl.when(ctx == j)
        def _():
            for part in range(3):
                first = part * 768 + DH * j
                head[:, DH * part : DH * (part + 1)] = held[:, first : first + DH]

    beta[240:336, :] = head[:, 0:128]
    beta[336:432, :] = head[:, 128:256]
    for g in range(3):
        beta[432:464, 32 * g : 32 * (g + 1)] = head[32 * g : 32 * (g + 1), 256:288]
    normed[...] = norm_rows(rows[...].astype(F32)).astype(BF16)


STEPS = (0, -1, -2, -3, 1, 2, 3)


def order_kernel(*refs):
    blocks, low, high, w, beta, gam = refs[0:7], refs[7], refs[8], refs[9], refs[10], refs[11]
    _, _, _, z, _, _ = whereabouts()

    def near(ref, at):
        for side in range(2):
            first = NEAR * side
            beta[at, 240 * side : 240 * (side + 1), :] = ref[first : first + 240, :]
            w[at, side, :, 0:128] = ref[first + 240 : first + 336, :]
            w[at, side, :, 128:256] = ref[first + 336 : first + 432, :]
            for g in range(3):
                w[at, side, 32 * g : 32 * (g + 1), 256:288] = ref[
                    first + 432 : first + 464, 32 * g : 32 * (g + 1)
                ]
            w[at, side, :, 288:384] = jnp.zeros((96, 96), BF16)

    near(low, z ^ 4)
    gam[z ^ 4] = high[...]
    for ref, step in zip(blocks, STEPS):
        at = (z + step) & 7
        near(ref, at)
        gam[at] = ref[2 * NEAR :, :]


def attend_kernel(length, x, w, out, q, k, v, att):
    att[0:HALO, :] = jnp.zeros((HALO, LANES), BF16)
    att[SEQ + HALO : SEQ + 2 * HALO, :] = jnp.zeros((HALO, LANES), BF16)
    for ref in (q, k, v):
        ref[:, DH:LANES] = jnp.zeros((SEQ, LANES - DH), BF16)
    mat = w[...].reshape(D, 3 * LANES)
    for i in range(4):
        rows = slice(256 * i, 256 * (i + 1))
        made = jnp.dot(x[2 * i : 2 * i + 2].reshape(256, D), mat, preferred_element_type=F32).astype(BF16)
        for part, ref in enumerate((q, k, v)):
            ref[rows, 0:DH] = made[:, DH * part : DH * (part + 1)]
    valid = lax.broadcasted_iota(jnp.int32, (1, SEQ), 1) < length[0]
    keys, values = k[...], v[...]
    for i in range(HEADS):
        scores = lax.dot_general(
            q[ROWS * i : ROWS * (i + 1), :], keys, (((1,), (1,)), ((), ())), preferred_element_type=F32
        )
        scores = jnp.where(valid, scores, masked_score)
        top = jnp.max(scores, axis=-1, keepdims=True)
        exp_scores = jnp.exp((scores - top) * DH ** (-0.5))
        total = jnp.sum(exp_scores, axis=-1, keepdims=True)
        added = jnp.dot(exp_scores.astype(BF16), values, preferred_element_type=F32)
        att[HALO + ROWS * i : HALO + ROWS * (i + 1), :] = (added / total).astype(BF16)
    for i in range(HEADS):
        out[i] = att[ROWS * i : ROWS * i + WIDE, :]


def cut_kernel(beta_1, beta_3, gamma_1, gamma_3, beta_low, beta_high, gamma_low, gamma_high, sems):
    run_copies(
        [
            (beta_1.at[0:4], beta_low), (beta_3.at[4:8], beta_high),
            (gamma_1.at[0:4], gamma_low), (gamma_3.at[4:8], gamma_high),
        ],
        sems,
    )()


def halves(refs):
    whole, low, high = slice(0, 8), slice(0, 4), slice(4, 8)
    return list(zip((0, 1, 2, 2, 3), (whole, whole, low, high, whole), refs))


def middle_kernel(length, att_in, frames_in, before_in, behind_in, taps_in, *refs):
    pieces = refs[0:20]
    out, att, frames, taps, heads, rows, w_out, w, w_conv, ext, summed, own_sems, out_sems, glu_sems, conv_sems = refs[20:]
    own_wait = run_copies(
        [
            (att_in, att), (before_in, frames.at[0:HALO]), (frames_in, frames.at[HALO : HALO + ROWS]),
            (behind_in, frames.at[HALO + ROWS :]), (taps_in, taps),
        ],
        own_sems,
    )
    _, y, a, _, h, core = whereabouts()
    owners = [(0, core), (10, 1 - core)]

    def glu_copy(source, z, rows, h, block):
        target = w.at[z, h, rows, columns(block)]
        pltpu.make_async_copy(source, target, glu_sems.at[block]).start()

    def conv_copy(source, z, rows, h, block):
        target = w_conv.at[z, h, rows, columns(block)]
        pltpu.make_async_copy(source, target, conv_sems.at[0]).start()

    def glu_wait(block):
        target = w.at[:, :, :, LANES * block : LANES * (block + 1)]
        pltpu.make_async_copy(target, target, glu_sems.at[block]).wait()

    copies = []
    for first, at in owners:
        for i, z, ref in halves(pieces[first : first + 5]):
            for side in range(2):
                start = 240 * side
                copies.append((ref.at[:, start : start + 48, :], w_out.at[z, side, :, columns(at * 6 + (y ^ i))]))
        for i, z, ref in halves(pieces[first + 5 : first + 10]):
            copies.append((ref.at[:, 0:48, :], w_out.at[z, h ^ (i >> 1), :, columns(at * 6 + 4 + (a ^ (i & 1)))]))
    out_wait = run_copies(copies, out_sems)
    whole, low, high = slice(0, 96), slice(0, 48), slice(48, 96)

    def start_beta():
        for first, at in owners:
            for i, z, ref in halves(pieces[first : first + 5]):
                for side in range(2):
                    start = 240 * side + 48
                    glu_copy(ref.at[:, start : start + 96, :], z, whole, side, at * 12 + (y ^ i))

    def start_mixed():
        for first, at in owners:
            for i, z, ref in halves(pieces[first : first + 5]):
                for side in range(2):
                    start = 240 * side + 144
                    glu_copy(ref.at[:, start : start + 48, :], z, low, side, at * 12 + 4 + (y ^ i))
            for i, z, ref in halves(pieces[first + 5 : first + 10]):
                block = at * 12 + 4 + 2 * (a ^ (i & 1))
                for j in range(2):
                    start = 48 + 48 * j
                    glu_copy(ref.at[:, start : start + 48, :], z, high, h ^ (i >> 1), block + j)

    def start_gamma():
        for first, at in owners:
            for i, z, ref in halves(pieces[first + 5 : first + 10]):
                block = at * 12 + 8 + 2 * (a ^ (i & 1))
                for j in range(2):
                    start = 144 + 96 * j
                    glu_copy(ref.at[:, start : start + 96, :], z, whole, h ^ (i >> 1), block + j)

    def start_conv():
        for first, at in owners:
            for i, z, ref in halves(pieces[first : first + 5]):
                for side in range(2):
                    start = 240 * side + 192
                    conv_copy(ref.at[:, start : start + 48, :], z, low, side, at * 6 + (y ^ i))
            for i, z, ref in halves(pieces[first + 5 : first + 10]):
                there = a ^ (i & 1)
                for j in range(2):
                    start = 336 + 48 * j
                    conv_copy(ref.at[:, start : start + 48, :], z, high, h ^ (i >> 1), at * 6 + 2 * there + j)
                conv_copy(ref.at[:, 432:528, :], z, whole, h ^ (i >> 1), at * 6 + 4 + there)

    start_beta()
    own_wait()
    for head in range(HEADS):
        heads[:, DH * head : DH * (head + 1)] = att[head, :, 0:DH]
    out_wait()
    for n in range(6):
        cols = slice(256 * n, 256 * (n + 1))
        mat = w_out[:, :, :, cols].reshape(HEADS * DH, 256)
        total = frames[:, cols].astype(F32) + jnp.dot(heads[...], mat, preferred_element_type=F32)
        frames[:, cols] = total.astype(BF16)
    start_mixed()
    for i in range(WIDE // 32):
        part = slice(32 * i, 32 * (i + 1))
        rows[part, :] = norm_rows(frames[part, :].astype(F32)).astype(BF16)

    position = lax.axis_index("ctx") * ROWS - HALO + lax.broadcasted_iota(jnp.int32, (WIDE, 1), 0)
    valid = (position >= 0) & (position < length[0])
    for n in range(6):
        for block in (2 * n, 2 * n + 1, 12 + 2 * n, 13 + 2 * n):
            glu_wait(block)
        mats = [
            w[:, :, :, at + 256 * n : at + 256 * (n + 1)].reshape(D, 256) for at in (0, D)
        ]
        value, gate = [jnp.dot(rows[...], mat, preferred_element_type=F32) for mat in mats]
        gated = value * jax.nn.sigmoid(gate)
        ext[:, 256 * n : 256 * (n + 1)] = jnp.where(valid, gated, 0.0).astype(BF16).astype(F32)
        if n == 0:
            start_gamma()
        if n == 2:
            start_conv()
        for m in (2 * n, 2 * n + 1):
            cols = slice(LANES * m, LANES * (m + 1))
            total = jnp.zeros((ROWS, LANES), F32)
            tap_rows = taps[:, cols].astype(F32)
            for r in range(8):
                moved = ext[r : r + ROWS + 24, cols]
                for k in range(4):
                    j = 8 * k + r - 1
                    if 0 <= j < TAPS:
                        total = total + tap_rows[j : j + 1, :] * moved[8 * k : 8 * k + ROWS]
            summed[:, cols] = total
    for i in range(ROWS // 16):
        part = slice(16 * i, 16 * (i + 1))
        normed = norm_rows(summed[part, :])
        rows[part, :] = (normed * jax.nn.sigmoid(normed)).astype(BF16)
    pltpu.make_async_copy(w_conv, w_conv, conv_sems.at[0]).wait()
    for n in range(6):
        cols = slice(256 * n, 256 * (n + 1))
        mat = w_conv[:, :, :, cols].reshape(D, 256)
        total = frames[HALO : HALO + ROWS, cols].astype(F32) + jnp.dot(
            rows[0:ROWS, :], mat, preferred_element_type=F32
        )
        out[:, cols] = total.astype(BF16)


def shape(*dims, dtype=BF16):
    return jax.ShapeDtypeStruct(dims, dtype)


def ring_z(own, low, high):
    below, above = [own], [own]
    for _ in range(3):
        below.append(send(below[-1], shift_z(1)))
        above.append(send(above[-1], shift_z(-1)))
    return below + above[1:] + [send(low(below[3]), shift_z(1)), send(high(above[3]), shift_z(-1))]


def per_device(frames, lengths, w_qkv, w_out, w_glu, depth_kernel, w_conv_out):
    frame_rows = frames[0]
    near, gamma, normed = pl.pallas_call(
        pack_kernel,
        out_shape=(shape(NEAR, LANES), shape(GAMMA, LANES), shape(ROWS, D)),
        in_specs=[ANY] * 5,
        out_specs=(VM,) * 3,
        scratch_shapes=[
            pltpu.VMEM((96, 2304), BF16), pltpu.VMEM((96, 384), BF16), pltpu.VMEM((ROWS, D), BF16),
            pltpu.SemaphoreType.DMA((14,)),
        ],
        compiler_params=params(),
    )(frame_rows, w_qkv, w_out, w_glu, w_conv_out)
    far = send(near, SWAP_H)
    every = lax.all_to_all(jnp.broadcast_to(normed[None], (8, ROWS, D)), "ctx", 0, 0)

    _, _, _, _, h, _ = whereabouts()
    pack = jnp.concatenate([jnp.where(h == 0, near, far), jnp.where(h == 0, far, near), gamma], axis=0)
    blocks = ring_z(pack, lambda v: v[: 2 * NEAR], lambda v: v[2 * NEAR :])
    w_head, beta, gamma = pl.pallas_call(
        order_kernel,
        out_shape=(shape(8, 2, 96, 3 * LANES), shape(8, BETA, LANES), shape(8, GAMMA, LANES)),
        in_specs=[VM] * 9,
        out_specs=(VM,) * 3,
        compiler_params=params(16),
    )(*blocks)

    gamma_1, gamma_3 = send(gamma, xor_x(1)), send(gamma, xor_x(3))
    beta_1, beta_3 = send(beta, xor_y(1)), send(beta, xor_y(3))
    beta_other, gamma_other = send(beta, SWAP_CORE), send(gamma, SWAP_CORE)

    att = pl.pallas_call(
        attend_kernel,
        out_shape=shape(8, WIDE, LANES),
        in_specs=[SM, VM, VM],
        out_specs=VM,
        scratch_shapes=[
            pltpu.VMEM((SEQ, LANES), BF16),
            pltpu.VMEM((SEQ, LANES), BF16),
            pltpu.VMEM((SEQ, LANES), BF16),
            pltpu.VMEM((SEQ + 2 * HALO, LANES), BF16),
        ],
        cost_estimate=cost(2 * 10**10),
        compiler_params=params(16),
    )(lengths, every, after(w_head, beta_other, gamma_other))

    up = [(i, i + 1) for i in range(7)]
    down = [(i + 1, i) for i in range(7)]
    halo = after(frame_rows, att)
    att = lax.all_to_all(att, "ctx", 0, 0)
    frames_before = lax.ppermute(halo[ROWS - HALO :], "ctx", up)
    frames_behind = lax.ppermute(halo[:HALO], "ctx", down)
    beta_1, beta_3, gamma_1, gamma_3, att, frames_before, frames_behind = lax.optimization_barrier(
        (beta_1, beta_3, gamma_1, gamma_3, att, frames_before, frames_behind)
    )
    beta_2, beta_2b, gamma_2, gamma_2b = pl.pallas_call(
        cut_kernel,
        out_shape=(shape(4, BETA, LANES),) * 2 + (shape(4, GAMMA, LANES),) * 2,
        in_specs=[ANY] * 4,
        out_specs=(VM,) * 4,
        scratch_shapes=[pltpu.SemaphoreType.DMA((4,))],
        compiler_params=params(16),
    )(beta_1, beta_3, gamma_1, gamma_3)
    beta_2, beta_2b = send(beta_2, xor_y(3)), send(beta_2b, xor_y(1))
    gamma_2, gamma_2b = send(gamma_2, xor_x(3)), send(gamma_2b, xor_x(1))
    swapped_1 = [send(v, SWAP_CORE) for v in (beta_1, beta_3, gamma_1, gamma_3)]
    second = [beta_2, beta_2b, gamma_2, gamma_2b]
    swapped_2 = [send(v, SWAP_CORE) for v in second]
    pieces = [
        beta, beta_1, beta_2, beta_2b, beta_3, gamma, gamma_1, gamma_2, gamma_2b, gamma_3,
        beta_other, swapped_1[0], swapped_2[0], swapped_2[1], swapped_1[1],
        gamma_other, swapped_1[2], swapped_2[2], swapped_2[3], swapped_1[3],
    ]

    result = pl.pallas_call(
        middle_kernel,
        out_shape=shape(ROWS, D),
        in_specs=[SM] + [ANY] * 25,
        out_specs=VM,
        scratch_shapes=[
            pltpu.VMEM((8, WIDE, LANES), BF16),
            pltpu.VMEM((WIDE, D), BF16),
            pltpu.VMEM((TAPS, D), BF16),
            pltpu.VMEM((WIDE, HEADS * DH), BF16),
            pltpu.VMEM((WIDE, D), BF16),
            pltpu.VMEM((8, 2, 48, D), BF16),
            pltpu.VMEM((8, 2, 96, 2 * D), BF16),
            pltpu.VMEM((8, 2, 96, D), BF16),
            pltpu.VMEM((WIDE, D), F32),
            pltpu.VMEM((ROWS, D), F32),
            pltpu.SemaphoreType.DMA((5,)),
            pltpu.SemaphoreType.DMA((30,)),
            pltpu.SemaphoreType.DMA((24,)),
            pltpu.SemaphoreType.DMA((1,)),
        ],
        compiler_params=params(26),
    )(lengths, att, frame_rows, frames_before, frames_behind, depth_kernel, *pieces)
    return result[None]


def solution(mesh):
    in_specs = (
        P(("dp", "fsdp"), "ctx", None),
        P(("dp", "fsdp")),
        P("fsdp", None),
        P("fsdp", None),
        P("fsdp", None),
        P(),
        P("fsdp", None),
    )
    out_specs = P(("dp", "fsdp"), "ctx", None)
    return jax.shard_map(
        per_device, mesh=mesh, in_specs=in_specs, out_specs=out_specs, check_vma=False
    )
```

```python
import numpy as np
import jax
import jax.numpy as jnp
from jax import lax
from jax.experimental import pallas as pl
from jax.experimental.pallas import tpu as pltpu
from jax.sharding import PartitionSpec as P

HEADS = 8
DH = 96
TAPS = 31
D = 1536
ROWS = 128
SEQ = 1024
LANES = 128
HALO = 16
WIDE = ROWS + 2 * HALO
masked_score = -1e30

AXES = ("ctx", "fsdp", "dp")
SHAPE = (2, 4, 8, 2, 2)
F32 = jnp.float32
BF16 = jnp.bfloat16


def pairs(move):
    out = []
    for i in range(256):
        c = [int(v) for v in np.unravel_index(i, SHAPE)]
        out.append((i, int(np.ravel_multi_index(move(*c), SHAPE))))
    return out


def xor_y(k):
    return pairs(lambda a, y, z, h, c: (a, y ^ k, z, h, c))


def xor_x(k):
    return pairs(lambda a, y, z, h, c: (a ^ (k & 1), y, z, h ^ (k >> 1), c))


def shift_z(k):
    return pairs(lambda a, y, z, h, c: (a, y, (z + k) % 8, h, c))


SWAP_CORE = pairs(lambda a, y, z, h, c: (a, y, z, h, 1 - c))
SWAP_H = pairs(lambda a, y, z, h, c: (a, y, z, 1 - h, c))

def send(value, moves):
    return lax.ppermute(value, AXES, moves)


def params(mib=60):
    return pltpu.CompilerParams(vmem_limit_bytes=mib * 2**20)


def cost(flops):
    return pl.CostEstimate(flops=flops, bytes_accessed=2**20, transcendentals=0)


def after(value, *others):
    return lax.optimization_barrier((value,) + others)[0]


def whereabouts():
    ctx, fsdp = lax.axis_index("ctx"), lax.axis_index("fsdp")
    return ctx, ctx & 3, ctx >> 2, fsdp >> 1, fsdp & 1, lax.axis_index("dp")


VM = pl.BlockSpec(memory_space=pltpu.VMEM)
SM = pl.BlockSpec(memory_space=pltpu.SMEM)
ANY = pl.BlockSpec(memory_space=pl.ANY)


def norm_rows(values):
    middle = jnp.mean(values, axis=-1, keepdims=True)
    apart = values - middle
    spread = jnp.mean(apart * apart, axis=-1, keepdims=True)
    return apart * lax.rsqrt(spread + 1e-05)


def columns(block, count=1):
    return pl.ds(pl.multiple_of(block * LANES, LANES), count * LANES)


def run_copies(copies, sems):
    made = [pltpu.make_async_copy(src, dst, sems.at[i]) for i, (src, dst) in enumerate(copies)]
    for copy in made:
        copy.start()

    def wait():
        for copy in made:
            copy.wait()

    return wait


BETA, GAMMA = 480, 528
NEAR = BETA // 2 + 224


def pack_kernel(x, w_qkv, w_out, w_glu, w_conv, beta, gam, every, held, head, rows, sems, send_sems):
    ctx, y, a, _, _, core = whereabouts()
    glu, conv = core * 12, core * 6
    copies = [
        (w_qkv, held),
        (x, rows),
        (w_out.at[:, columns(conv + y)], beta.at[0:48, :]),
        (w_glu.at[:, columns(glu + y)], beta.at[48:144, :]),
        (w_glu.at[0:48, columns(glu + 4 + y)], beta.at[144:192, :]),
        (w_conv.at[0:48, columns(conv + y)], beta.at[192:240, :]),
        (w_out.at[:, columns(conv + 4 + a)], gam.at[0:48, :]),
        (w_conv.at[:, columns(conv + 4 + a)], gam.at[432:528, :]),
    ]
    for j in range(2):
        copies.append((w_glu.at[48:96, columns(glu + 4 + 2 * a + j)], gam.at[48 + 48 * j : 96 + 48 * j, :]))
        copies.append((w_glu.at[:, columns(glu + 8 + 2 * a + j)], gam.at[144 + 96 * j : 240 + 96 * j, :]))
        copies.append((w_conv.at[48:96, columns(conv + 2 * a + j)], gam.at[336 + 48 * j : 384 + 48 * j, :]))
    wait = run_copies(copies, sems)
    beta[432:464, :] = jnp.zeros((32, LANES), BF16)
    wait()
    rows[...] = norm_rows(rows[...].astype(F32)).astype(BF16)
    sent = run_copies([(rows, every.at[i]) for i in range(8)], send_sems)
    for j in range(HEADS):

        @pl.when(ctx == j)
        def _():
            for part in range(3):
                first = part * 768 + DH * j
                head[:, DH * part : DH * (part + 1)] = held[:, first : first + DH]

    beta[240:336, :] = head[:, 0:128]
    beta[336:432, :] = head[:, 128:256]
    for g in range(3):
        beta[432:464, 32 * g : 32 * (g + 1)] = head[32 * g : 32 * (g + 1), 256:288]
    sent()


STEPS = (0, -1, -2, -3, 1, 2, 3)


def order_kernel(*refs):
    blocks, low, high, w, beta, gam = refs[0:7], refs[7], refs[8], refs[9], refs[10], refs[11]
    _, _, _, z, _, _ = whereabouts()

    def near(ref, at):
        for side in range(2):
            first = NEAR * side
            beta[at, 240 * side : 240 * (side + 1), :] = ref[first : first + 240, :]
            w[at, side, :, 0:128] = ref[first + 240 : first + 336, :]
            w[at, side, :, 128:256] = ref[first + 336 : first + 432, :]
            for g in range(3):
                w[at, side, 32 * g : 32 * (g + 1), 256:288] = ref[
                    first + 432 : first + 464, 32 * g : 32 * (g + 1)
                ]
            w[at, side, :, 288:384] = jnp.zeros((96, 96), BF16)

    near(low, z ^ 4)
    gam[z ^ 4] = high[...]
    for ref, step in zip(blocks, STEPS):
        at = (z + step) & 7
        near(ref, at)
        gam[at] = ref[2 * NEAR :, :]


def attend_kernel(length, x, w, out, q, k, v, att):
    att[0:HALO, :] = jnp.zeros((HALO, LANES), BF16)
    att[SEQ + HALO : SEQ + 2 * HALO, :] = jnp.zeros((HALO, LANES), BF16)
    for ref in (q, k, v):
        ref[:, DH:LANES] = jnp.zeros((SEQ, LANES - DH), BF16)
    mat = w[...].reshape(D, 3 * LANES)
    for i in range(4):
        rows = slice(256 * i, 256 * (i + 1))
        made = jnp.dot(x[2 * i : 2 * i + 2].reshape(256, D), mat, preferred_element_type=F32).astype(BF16)
        for part, ref in enumerate((q, k, v)):
            ref[rows, 0:DH] = made[:, DH * part : DH * (part + 1)]
    valid = lax.broadcasted_iota(jnp.int32, (1, SEQ), 1) < length[0]
    keys, values = k[...], v[...]
    for i in range(HEADS):
        scores = lax.dot_general(
            q[ROWS * i : ROWS * (i + 1), :], keys, (((1,), (1,)), ((), ())), preferred_element_type=F32
        )
        scores = jnp.where(valid, scores, masked_score)
        top = jnp.max(scores, axis=-1, keepdims=True)
        exp_scores = jnp.exp((scores - top) * DH ** (-0.5))
        total = jnp.sum(exp_scores, axis=-1, keepdims=True)
        added = jnp.dot(exp_scores.astype(BF16), values, preferred_element_type=F32)
        att[HALO + ROWS * i : HALO + ROWS * (i + 1), :] = (added / total).astype(BF16)
    for i in range(HEADS):
        out[i] = att[ROWS * i : ROWS * i + WIDE, :]


def cut_kernel(beta_1, beta_3, gamma_1, gamma_3, beta_low, beta_high, gamma_low, gamma_high, sems):
    run_copies(
        [
            (beta_1.at[0:4], beta_low), (beta_3.at[4:8], beta_high),
            (gamma_1.at[0:4], gamma_low), (gamma_3.at[4:8], gamma_high),
        ],
        sems,
    )()


def halves(refs):
    whole, low, high = slice(0, 8), slice(0, 4), slice(4, 8)
    return list(zip((0, 1, 2, 2, 3), (whole, whole, low, high, whole), refs))


def middle_kernel(length, att_in, frames_in, before_in, behind_in, taps_in, *refs):
    pieces = refs[0:20]
    out, att, frames, taps, heads, rows, w_out, w, w_conv, ext, summed, own_sems, out_sems, glu_sems, conv_sems = refs[20:]
    own_wait = run_copies(
        [
            (att_in, att), (before_in, frames.at[0:HALO]), (frames_in, frames.at[HALO : HALO + ROWS]),
            (behind_in, frames.at[HALO + ROWS :]), (taps_in, taps),
        ],
        own_sems,
    )
    _, y, a, _, h, core = whereabouts()
    owners = [(0, core), (10, 1 - core)]

    def glu_copy(source, z, rows, h, block):
        target = w.at[z, h, rows, columns(block)]
        pltpu.make_async_copy(source, target, glu_sems.at[block]).start()

    def conv_copy(source, z, rows, h, block):
        target = w_conv.at[z, h, rows, columns(block)]
        pltpu.make_async_copy(source, target, conv_sems.at[0]).start()

    def glu_wait(block):
        target = w.at[:, :, :, LANES * block : LANES * (block + 1)]
        pltpu.make_async_copy(target, target, glu_sems.at[block]).wait()

    copies = []
    for first, at in owners:
        for i, z, ref in halves(pieces[first : first + 5]):
            for side in range(2):
                start = 240 * side
                copies.append((ref.at[:, start : start + 48, :], w_out.at[z, side, :, columns(at * 6 + (y ^ i))]))
        for i, z, ref in halves(pieces[first + 5 : first + 10]):
            copies.append((ref.at[:, 0:48, :], w_out.at[z, h ^ (i >> 1), :, columns(at * 6 + 4 + (a ^ (i & 1)))]))
    out_wait = run_copies(copies, out_sems)
    whole, low, high = slice(0, 96), slice(0, 48), slice(48, 96)

    def start_beta():
        for first, at in owners:
            for i, z, ref in halves(pieces[first : first + 5]):
                for side in range(2):
                    start = 240 * side + 48
                    glu_copy(ref.at[:, start : start + 96, :], z, whole, side, at * 12 + (y ^ i))

    def start_mixed():
        for first, at in owners:
            for i, z, ref in halves(pieces[first : first + 5]):
                for side in range(2):
                    start = 240 * side + 144
                    glu_copy(ref.at[:, start : start + 48, :], z, low, side, at * 12 + 4 + (y ^ i))
            for i, z, ref in halves(pieces[first + 5 : first + 10]):
                block = at * 12 + 4 + 2 * (a ^ (i & 1))
                for j in range(2):
                    start = 48 + 48 * j
                    glu_copy(ref.at[:, start : start + 48, :], z, high, h ^ (i >> 1), block + j)

    def start_gamma():
        for first, at in owners:
            for i, z, ref in halves(pieces[first + 5 : first + 10]):
                block = at * 12 + 8 + 2 * (a ^ (i & 1))
                for j in range(2):
                    start = 144 + 96 * j
                    glu_copy(ref.at[:, start : start + 96, :], z, whole, h ^ (i >> 1), block + j)

    def start_conv():
        for first, at in owners:
            for i, z, ref in halves(pieces[first : first + 5]):
                for side in range(2):
                    start = 240 * side + 192
                    conv_copy(ref.at[:, start : start + 48, :], z, low, side, at * 6 + (y ^ i))
            for i, z, ref in halves(pieces[first + 5 : first + 10]):
                there = a ^ (i & 1)
                for j in range(2):
                    start = 336 + 48 * j
                    conv_copy(ref.at[:, start : start + 48, :], z, high, h ^ (i >> 1), at * 6 + 2 * there + j)
                conv_copy(ref.at[:, 432:528, :], z, whole, h ^ (i >> 1), at * 6 + 4 + there)

    start_beta()
    own_wait()
    for head in range(HEADS):
        heads[:, DH * head : DH * (head + 1)] = att[head, :, 0:DH]
    out_wait()
    for n in range(6):
        cols = slice(256 * n, 256 * (n + 1))
        mat = w_out[:, :, :, cols].reshape(HEADS * DH, 256)
        total = frames[:, cols].astype(F32) + jnp.dot(heads[...], mat, preferred_element_type=F32)
        frames[:, cols] = total.astype(BF16)
    start_mixed()
    for i in range(WIDE // 32):
        part = slice(32 * i, 32 * (i + 1))
        rows[part, :] = norm_rows(frames[part, :].astype(F32)).astype(BF16)

    position = lax.axis_index("ctx") * ROWS - HALO + lax.broadcasted_iota(jnp.int32, (WIDE, 1), 0)
    valid = (position >= 0) & (position < length[0])
    for n in range(6):
        for block in (2 * n, 2 * n + 1, 12 + 2 * n, 13 + 2 * n):
            glu_wait(block)
        mats = [
            w[:, :, :, at + 256 * n : at + 256 * (n + 1)].reshape(D, 256) for at in (0, D)
        ]
        value, gate = [jnp.dot(rows[...], mat, preferred_element_type=F32) for mat in mats]
        gated = value * jax.nn.sigmoid(gate)
        ext[:, 256 * n : 256 * (n + 1)] = jnp.where(valid, gated, 0.0).astype(BF16).astype(F32)
        if n == 0:
            start_gamma()
        if n == 2:
            start_conv()
        for m in (2 * n, 2 * n + 1):
            cols = slice(LANES * m, LANES * (m + 1))
            total = jnp.zeros((ROWS, LANES), F32)
            tap_rows = taps[:, cols].astype(F32)
            for r in range(8):
                moved = ext[r : r + ROWS + 24, cols]
                for k in range(4):
                    j = 8 * k + r - 1
                    if 0 <= j < TAPS:
                        total = total + tap_rows[j : j + 1, :] * moved[8 * k : 8 * k + ROWS]
            summed[:, cols] = total
    for i in range(ROWS // 16):
        part = slice(16 * i, 16 * (i + 1))
        normed = norm_rows(summed[part, :])
        rows[part, :] = (normed * jax.nn.sigmoid(normed)).astype(BF16)
    pltpu.make_async_copy(w_conv, w_conv, conv_sems.at[0]).wait()
    for n in range(6):
        cols = slice(256 * n, 256 * (n + 1))
        mat = w_conv[:, :, :, cols].reshape(D, 256)
        total = frames[HALO : HALO + ROWS, cols].astype(F32) + jnp.dot(
            rows[0:ROWS, :], mat, preferred_element_type=F32
        )
        out[:, cols] = total.astype(BF16)


def shape(*dims, dtype=BF16):
    return jax.ShapeDtypeStruct(dims, dtype)


def ring_z(own, low, high):
    below, above = [own], [own]
    for _ in range(3):
        below.append(send(below[-1], shift_z(1)))
        above.append(send(above[-1], shift_z(-1)))
    return below + above[1:] + [send(low(below[3]), shift_z(1)), send(high(above[3]), shift_z(-1))]


def per_device(frames, lengths, w_qkv, w_out, w_glu, depth_kernel, w_conv_out):
    frame_rows = frames[0]
    near, gamma, own_frames = pl.pallas_call(
        pack_kernel,
        out_shape=(shape(NEAR, LANES), shape(GAMMA, LANES), shape(8, ROWS, D)),
        in_specs=[ANY] * 5,
        out_specs=(VM, VM, ANY),
        scratch_shapes=[
            pltpu.VMEM((96, 2304), BF16), pltpu.VMEM((96, 384), BF16), pltpu.VMEM((ROWS, D), BF16),
            pltpu.SemaphoreType.DMA((14,)), pltpu.SemaphoreType.DMA((8,)),
        ],
        compiler_params=params(),
    )(frame_rows, w_qkv, w_out, w_glu, w_conv_out)
    far = send(near, SWAP_H)
    every = lax.all_to_all(own_frames, "ctx", 0, 0)

    _, _, _, _, h, _ = whereabouts()
    pack = jnp.concatenate([jnp.where(h == 0, near, far), jnp.where(h == 0, far, near), gamma], axis=0)
    blocks = ring_z(pack, lambda v: v[: 2 * NEAR], lambda v: v[2 * NEAR :])
    w_head, beta, gamma = pl.pallas_call(
        order_kernel,
        out_shape=(shape(8, 2, 96, 3 * LANES), shape(8, BETA, LANES), shape(8, GAMMA, LANES)),
        in_specs=[VM] * 9,
        out_specs=(VM,) * 3,
        compiler_params=params(16),
    )(*blocks)

    gamma_1, gamma_3 = send(gamma, xor_x(1)), send(gamma, xor_x(3))
    beta_1, beta_3 = send(beta, xor_y(1)), send(beta, xor_y(3))
    beta_other, gamma_other = send(beta, SWAP_CORE), send(gamma, SWAP_CORE)

    att = pl.pallas_call(
        attend_kernel,
        out_shape=shape(8, WIDE, LANES),
        in_specs=[SM, VM, VM],
        out_specs=VM,
        scratch_shapes=[
            pltpu.VMEM((SEQ, LANES), BF16),
            pltpu.VMEM((SEQ, LANES), BF16),
            pltpu.VMEM((SEQ, LANES), BF16),
            pltpu.VMEM((SEQ + 2 * HALO, LANES), BF16),
        ],
        cost_estimate=cost(2 * 10**10),
        compiler_params=params(16),
    )(lengths, every, after(w_head, beta_other, gamma_other))

    up = [(i, i + 1) for i in range(7)]
    down = [(i + 1, i) for i in range(7)]
    halo = after(frame_rows, att)
    att = lax.all_to_all(att, "ctx", 0, 0)
    frames_before = lax.ppermute(halo[ROWS - HALO :], "ctx", up)
    frames_behind = lax.ppermute(halo[:HALO], "ctx", down)
    beta_1, beta_3, gamma_1, gamma_3, att, frames_before, frames_behind = lax.optimization_barrier(
        (beta_1, beta_3, gamma_1, gamma_3, att, frames_before, frames_behind)
    )
    beta_2, beta_2b, gamma_2, gamma_2b = pl.pallas_call(
        cut_kernel,
        out_shape=(shape(4, BETA, LANES),) * 2 + (shape(4, GAMMA, LANES),) * 2,
        in_specs=[ANY] * 4,
        out_specs=(VM,) * 4,
        scratch_shapes=[pltpu.SemaphoreType.DMA((4,))],
        compiler_params=params(16),
    )(beta_1, beta_3, gamma_1, gamma_3)
    beta_2, beta_2b = send(beta_2, xor_y(3)), send(beta_2b, xor_y(1))
    gamma_2, gamma_2b = send(gamma_2, xor_x(3)), send(gamma_2b, xor_x(1))
    swapped_1 = [send(v, SWAP_CORE) for v in (beta_1, beta_3, gamma_1, gamma_3)]
    second = [beta_2, beta_2b, gamma_2, gamma_2b]
    swapped_2 = [send(v, SWAP_CORE) for v in second]
    pieces = [
        beta, beta_1, beta_2, beta_2b, beta_3, gamma, gamma_1, gamma_2, gamma_2b, gamma_3,
        beta_other, swapped_1[0], swapped_2[0], swapped_2[1], swapped_1[1],
        gamma_other, swapped_1[2], swapped_2[2], swapped_2[3], swapped_1[3],
    ]

    result = pl.pallas_call(
        middle_kernel,
        out_shape=shape(ROWS, D),
        in_specs=[SM] + [ANY] * 25,
        out_specs=VM,
        scratch_shapes=[
            pltpu.VMEM((8, WIDE, LANES), BF16),
            pltpu.VMEM((WIDE, D), BF16),
            pltpu.VMEM((TAPS, D), BF16),
            pltpu.VMEM((WIDE, HEADS * DH), BF16),
            pltpu.VMEM((WIDE, D), BF16),
            pltpu.VMEM((8, 2, 48, D), BF16),
            pltpu.VMEM((8, 2, 96, 2 * D), BF16),
            pltpu.VMEM((8, 2, 96, D), BF16),
            pltpu.VMEM((WIDE, D), F32),
            pltpu.VMEM((ROWS, D), F32),
            pltpu.SemaphoreType.DMA((5,)),
            pltpu.SemaphoreType.DMA((30,)),
            pltpu.SemaphoreType.DMA((24,)),
            pltpu.SemaphoreType.DMA((1,)),
        ],
        compiler_params=params(26),
    )(lengths, att, frame_rows, frames_before, frames_behind, depth_kernel, *pieces)
    return result[None]


def solution(mesh):
    in_specs = (
        P(("dp", "fsdp"), "ctx", None),
        P(("dp", "fsdp")),
        P("fsdp", None),
        P("fsdp", None),
        P("fsdp", None),
        P(),
        P("fsdp", None),
    )
    out_specs = P(("dp", "fsdp"), "ctx", None)
    return jax.shard_map(
        per_device, mesh=mesh, in_specs=in_specs, out_specs=out_specs, check_vma=False
    )
```
